256 devices in a mesh: ctx: 32 (over y, z_lo, core), kvh: 8 (over z_hi, x).
Axes of the slice: x: 4, y: 4, z: 8 (z_hi: 2, z_lo: 4; z = z_hi * 4 + z_lo), core: 2. Of those that a mesh axis runs over, the one named last changes fastest.
Arguments:
- queries: bfloat16 [3072, 8192], P('ctx', 'kvh'), may hold values from -360 to 360
- cache_keys: bfloat16 [16384, 1024], P('ctx', 'kvh'), may hold values from -6 to 6
- cache_values: bfloat16 [16384, 1024], P('ctx', 'kvh'), may hold values from -12 to 12
- test_keys: bfloat16 [3072, 1024], P('ctx', 'kvh'), may hold values from -10 to 10
- test_values: bfloat16 [3072, 1024], P('ctx', 'kvh'), may hold values from -12 to 12
- window_select: int32 [96, 16], replicated, may hold values 0 or 1
- test_lengths: int32 [96], replicated, may hold values from 1 to 32, 1536 in all
- out_weight: bfloat16 [8192, 8192], P('kvh', 'ctx'), may hold values from -0.0625 to 0.0625
Outputs:
- projected: bfloat16 [3072, 8192], P('kvh', 'ctx')
The draws below stay inside these ranges and needn't reach their ends.
All inputs are finite; a program needn't handle non-finite values.
Results may differ from the reference program's by a relative error of at most 0.012.
Values may be sent and summed in bfloat16 or wider, within the bound.
No kernel may reach another device: no remote copies, remote signals or barrier semaphores. Data moves between devices by JAX's collectives and lax.ppermute only.
A program may use at most 128 MiB of HBM per device.

```python
import math
import jax
import jax.numpy as jnp
import numpy as np
from jax import lax

D = 8192
Q_HEADS = 64
KV_HEADS = 8
HEAD_DIM = 128
GROUP = 8
TOK_DEV = 512
WINDOWS = 16
TLEN = 32
CTX_TOKENS = 16384
EXAMPLES = 96
ROWS = 3072
N_CTX = 32


def shared_draw(key):
    cache_part = jnp.clip(jax.random.normal(jax.random.fold_in(key, 11), (CTX_TOKENS, KV_HEADS * HEAD_DIM), jnp.float32), -6.0, 6.0)
    test_part = 1.6 * jnp.clip(jax.random.normal(jax.random.fold_in(key, 12), (ROWS, KV_HEADS * HEAD_DIM), jnp.float32), -6.0, 6.0)
    query_part = 3.0 * jnp.clip(jax.random.normal(jax.random.fold_in(key, 13), (ROWS, Q_HEADS * HEAD_DIM), jnp.float32), -6.0, 6.0)
    return (cache_part, test_part, query_part)


def draw_queries(key, part):
    cache_part, test_part, query_part = shared_draw(key)
    return query_part.astype(jnp.bfloat16)


def draw_cache_keys(key, part):
    cache_part, test_part, query_part = shared_draw(key)
    return cache_part.astype(jnp.bfloat16)


def draw_test_keys(key, part):
    cache_part, test_part, query_part = shared_draw(key)
    return test_part.astype(jnp.bfloat16)


def plant(result, stream_key, low, largest):
    spot = [jax.random.randint(jax.random.fold_in(stream_key, axis), (), 0, length) for axis, length in enumerate(result.shape)]
    longest = result.shape.index(max(result.shape))
    neighbour = spot[:longest] + [(spot[longest] + 1) % result.shape[longest]] + spot[longest + 1:]
    return result.at[tuple(spot)].set(low).at[tuple(neighbour)].set(largest)


def levels(key, extent, cuts, low, largest):
    gain, own = 1.0, jax.random.fold_in(key, 6)
    for position, blocks in cuts:
        steps = jnp.exp(jax.random.uniform(jax.random.fold_in(own, position), (blocks,), jnp.float32, low / len(cuts), largest / len(cuts)))
        gain = gain * jnp.repeat(steps, extent[position] // blocks).reshape([-1 if axis == position else 1 for axis in range(len(extent))])
    return gain


def length_profile(count, total, most, slope):
    weights = [(1 << 20) // math.isqrt(grade ** slope) + 1 for grade in range(2, count + 1)]
    rest, counts = total - most - (count - 1), [1] * (count - 1)
    while rest > 0:
        free = [i for i in range(count - 1) if counts[i] < most]
        pool, left = sum([weights[i] for i in free]), rest
        for i in free:
            extra = min(most - counts[i], max(1, left * weights[i] // pool), rest)
            counts[i] = counts[i] + extra
            rest = rest - extra
    return np.array([most] + counts)


def uneven(own_key, number_of, total, bound, skew):
    if number_of == 2:
        one = jax.random.randint(own_key, (), max(1, total - bound), min(bound, total - 1) + 1)
        return jnp.stack([one, total - one])
    lengths = jnp.asarray(length_profile(number_of, total, bound, skew), jnp.int32)
    couples = (number_of - 1) // 2
    source_of, taker = lengths[1:1 + 2 * couples:2], lengths[2:2 + 2 * couples:2]
    slack = jnp.minimum(source_of - 1, bound - taker)
    passed = jax.random.randint(jax.random.fold_in(own_key, 1), (couples,), 0, 1 << 20) % (slack + 1)
    lengths = lengths.at[1:1 + 2 * couples:2].set(source_of - passed).at[2:2 + 2 * couples:2].set(taker + passed)
    return lengths[jax.random.permutation(jax.random.fold_in(own_key, 2), number_of)]


def scatter_about(stream_key, extent, scale, limit, split=(), kind=jnp.bfloat16):
    factor_of = levels(stream_key, extent, split, -0.22, 0.18) if split else 1.0
    entries = jax.random.normal(stream_key, extent, jnp.float32) * scale * factor_of
    return jnp.minimum(jnp.maximum(entries, -limit), limit).astype(kind)


def setup_inputs(seed: int = 0) -> dict:
    streams_of = jax.random.split(jax.random.key(seed), 9)
    queries = draw_queries(jax.random.fold_in(streams_of[8], 71), 0)
    cache_keys = draw_cache_keys(jax.random.fold_in(streams_of[8], 71), 0)
    cache_values = scatter_about(streams_of[2], (CTX_TOKENS, KV_HEADS * HEAD_DIM), 2.0, 12.0, ((0, 32), (1, 8)))
    test_keys = draw_test_keys(jax.random.fold_in(streams_of[8], 71), 0)
    test_values = scatter_about(streams_of[4], (ROWS, KV_HEADS * HEAD_DIM), 2.0, 12.0, ((0, 32), (1, 8)))
    window_select = plant((jax.random.randint(streams_of[5], (EXAMPLES, WINDOWS), 0, 4) < 3).astype(jnp.int32), jax.random.fold_in(streams_of[5], 1), 0, 1)
    test_lengths = uneven(streams_of[6], EXAMPLES, EXAMPLES * TLEN // 2, TLEN, 2).astype(jnp.int32)
    out_weight = scatter_about(streams_of[7], (D, D), D ** -0.5, 0.0625, ((0, 8), (1, 32)))
    return dict(queries=queries, cache_keys=cache_keys, cache_values=cache_values, test_keys=test_keys, test_values=test_values, window_select=window_select, test_lengths=test_lengths, out_weight=out_weight)


NEG_FILL = -1e+30

def allowed_mask(row_start, row_count, tok_start, tok_count, window_select, window_len):
    row_ids = row_start + jnp.arange(row_count, dtype=jnp.int32)
    example_ids = row_ids // TLEN
    example_hot = (example_ids[:, None] == jnp.arange(window_select.shape[0], dtype=jnp.int32)[None, :]).astype(jnp.float32)
    row_windows = jnp.dot(example_hot, window_select.astype(jnp.float32))
    token_ids = tok_start + jnp.arange(tok_count, dtype=jnp.int32)
    window_hot = ((token_ids // window_len)[:, None] == jnp.arange(window_select.shape[1], dtype=jnp.int32)[None, :]).astype(jnp.float32)
    return jnp.dot(row_windows, window_hot.T) > 0.5

def attend_block(query_rows, key_rows, value_rows, allowed):
    row_count = query_rows.shape[0]
    tok_count = key_rows.shape[0]
    kv_count = key_rows.shape[1] // HEAD_DIM
    query_heads = query_rows.astype(jnp.float32).reshape(row_count, kv_count, GROUP, HEAD_DIM)
    key_heads = key_rows.astype(jnp.float32).reshape(tok_count, kv_count, HEAD_DIM)
    value_heads = value_rows.astype(jnp.float32).reshape(tok_count, kv_count, HEAD_DIM)
    scores = jnp.einsum('nkgd,tkd->nkgt', query_heads, key_heads) * (1.0 / math.sqrt(HEAD_DIM))
    visible = allowed[:, None, None, :]
    row_max = lax.optimization_barrier(jnp.max(jnp.where(visible, scores, NEG_FILL), axis=-1))
    row_max = lax.optimization_barrier(row_max.astype(jnp.bfloat16)).astype(jnp.float32)
    weights = jnp.where(visible, jnp.exp(scores - row_max[..., None]), 0.0)
    totals = lax.optimization_barrier(jnp.sum(weights, axis=-1))
    totals = lax.optimization_barrier(totals.astype(jnp.bfloat16)).astype(jnp.float32)
    rounded = lax.optimization_barrier(weights.astype(jnp.bfloat16))
    weighted = jnp.einsum('nkgt,tkd->nkgd', rounded.astype(jnp.float32), value_heads)
    outputs = (weighted / jnp.maximum(totals, 0.5)[..., None]).astype(jnp.bfloat16)
    return (outputs.reshape(row_count, -1), row_max.reshape(row_count, -1), totals.reshape(row_count, -1))

def finish(window_max, window_total, window_accum, prefix_out, prefix_max, prefix_total, live):
    row_count = prefix_out.shape[0]
    joint = jnp.maximum(window_max, prefix_max)
    window_scale = jnp.exp(window_max - joint)
    prefix_scale = jnp.exp(prefix_max - joint) * prefix_total
    prefix_heads = prefix_out.reshape(row_count, -1, HEAD_DIM).astype(jnp.float32)
    weighted = window_scale[..., None] * window_accum + prefix_scale[..., None] * prefix_heads
    denom = window_scale * window_total + prefix_scale
    attention = (weighted / denom[..., None]).reshape(row_count, -1)
    return jnp.where(live[:, None], attention, 0.0).astype(jnp.bfloat16)

def reference(queries, cache_keys, cache_values, test_keys, test_values, window_select, test_lengths, out_weight):
    row_total = queries.shape[0]
    window_len = CTX_TOKENS // WINDOWS
    key_blocks = cache_keys.reshape(N_CTX, TOK_DEV, -1)
    value_blocks = cache_values.reshape(N_CTX, TOK_DEV, -1)

    def absorb(carry, block):
        run_max, run_total, run_accum = carry
        index, key_rows, value_rows = block
        allowed = allowed_mask(jnp.int32(0), row_total, index * TOK_DEV, TOK_DEV, window_select, window_len)
        outputs, block_max, block_total = attend_block(queries, key_rows, value_rows, allowed)
        joint = jnp.maximum(run_max, block_max)
        old_scale = jnp.exp(run_max - joint)
        new_scale = jnp.exp(block_max - joint) * block_total
        heads_out = outputs.reshape(row_total, Q_HEADS, HEAD_DIM).astype(jnp.float32)
        run_accum = old_scale[..., None] * run_accum + new_scale[..., None] * heads_out
        run_total = old_scale * run_total + new_scale
        return ((joint, run_total, run_accum), None)
    start_state = (jnp.full((row_total, Q_HEADS), NEG_FILL, jnp.float32), jnp.zeros((row_total, Q_HEADS), jnp.float32), jnp.zeros((row_total, Q_HEADS, HEAD_DIM), jnp.float32))
    (window_max, window_total, window_accum), _ = lax.scan(absorb, start_state, (jnp.arange(N_CTX, dtype=jnp.int32), key_blocks, value_blocks))
    causal = jnp.arange(TLEN)[:, None] >= jnp.arange(TLEN)[None, :]
    prefix_out, prefix_max, prefix_total = jax.vmap(attend_block, in_axes=(0, 0, 0, None))(queries.reshape(EXAMPLES, TLEN, -1), test_keys.reshape(EXAMPLES, TLEN, -1), test_values.reshape(EXAMPLES, TLEN, -1), causal)
    prefix_out = prefix_out.reshape(row_total, -1)
    prefix_max = prefix_max.reshape(row_total, -1)
    prefix_total = prefix_total.reshape(row_total, -1)
    positions = jnp.arange(row_total, dtype=jnp.int32) % TLEN
    row_lengths = jnp.repeat(test_lengths, TLEN)
    live = positions < row_lengths
    attention = finish(window_max, window_total, window_accum, prefix_out, prefix_max, prefix_total, live)
    return jnp.dot(attention, out_weight, preferred_element_type=jnp.float32).astype(jnp.bfloat16)
```

```python
import functools
import math

import jax
import jax.numpy as jnp
from jax import lax
from jax.experimental import pallas as pl
from jax.experimental.pallas import tpu as pltpu
from jax.sharding import PartitionSpec as P

HEAD_DIM = 128
GROUP = 8
WINDOWS = 16
TLEN = 32
COLS = TLEN * GROUP
NEG_FILL = -1e30
SCALE = 1.0 / math.sqrt(HEAD_DIM)
LOG2E = math.log2(math.e)


def example_columns(q_ref, e):
    rows = q_ref[e * TLEN : (e + 1) * TLEN, :]
    return jnp.concatenate(
        [rows[:, h * HEAD_DIM : (h + 1) * HEAD_DIM] for h in range(GROUP)], axis=0
    )


def weigh(keys, values_t, columns, mask=None):
    dots = lax.dot_general(
        keys, columns, (((1,), (1,)), ((), ())), preferred_element_type=jnp.float32
    )
    if mask is not None:
        dots = jnp.where(mask, dots, NEG_FILL)
    top = jnp.max(dots, axis=0, keepdims=True) * SCALE
    top = top.astype(jnp.bfloat16).astype(jnp.float32)
    weights = jnp.exp2(dots * (SCALE * LOG2E) - top * LOG2E)
    if mask is not None:
        weights = jnp.where(mask, weights, 0.0)
    total = jnp.sum(weights, axis=0, keepdims=True)
    total = total.astype(jnp.bfloat16).astype(jnp.float32)
    out = jnp.dot(values_t, weights.astype(jnp.bfloat16), preferred_element_type=jnp.float32)
    out = out * (1.0 / jnp.maximum(total, 0.5))
    return top, total, out.astype(jnp.bfloat16).astype(jnp.float32)


def attention_kernel(
    examples, select_ref, length_ref, q_ref, tk_ref, tv_ref, kv_ref, out_ref, top_ref, total_ref, sum_ref
):
    step = pl.program_id(0)

    @pl.when(step == 0)
    def _():
        token = lax.broadcasted_iota(jnp.int32, (TLEN, COLS), 0)
        place = lax.broadcasted_iota(jnp.int32, (TLEN, COLS), 1) % TLEN
        for e in range(examples):
            rows = pl.ds(e * TLEN, TLEN)
            top, total, out = weigh(
                tk_ref[rows, :],
                tv_ref[rows, :].astype(jnp.float32).T.astype(jnp.bfloat16),
                example_columns(q_ref, e),
                token <= place,
            )
            top_ref[e] = top
            total_ref[e] = total
            sum_ref[e] = total * out

    keys = kv_ref[:, :HEAD_DIM]
    values_t = kv_ref[:, HEAD_DIM:].astype(jnp.float32).T.astype(jnp.bfloat16)
    for e in range(examples):
        top, total, out = weigh(keys, values_t, example_columns(q_ref, e))
        seen = select_ref[e, step] > 0
        top = jnp.where(seen, top, NEG_FILL)
        total = jnp.where(seen, total, 0.0)
        joint = jnp.maximum(top_ref[e], top)
        old = jnp.exp(top_ref[e] - joint)
        new = jnp.exp(top - joint) * total
        top_ref[e] = joint
        total_ref[e] = old * total_ref[e] + new
        sum_ref[e] = old * sum_ref[e] + new * out

    @pl.when(step == pl.num_programs(0) - 1)
    def _():
        place = lax.broadcasted_iota(jnp.int32, (1, COLS), 1) % TLEN
        for e in range(examples):
            live = place < length_ref[e]
            result = jnp.where(live, sum_ref[e] / total_ref[e], 0.0).T
            for h in range(GROUP):
                out_ref[e * TLEN : (e + 1) * TLEN, h * HEAD_DIM : (h + 1) * HEAD_DIM] = result[
                    h * TLEN : (h + 1) * TLEN, :
                ].astype(jnp.bfloat16)


def attend(queries, test_keys, test_values, cache, select, lengths, tok_dev):
    rows, width = queries.shape
    examples = rows // TLEN
    blocks = cache.shape[0] // tok_dev
    whole = lambda shape: pl.BlockSpec(shape, lambda b: (0, 0))
    return pl.pallas_call(
        functools.partial(attention_kernel, examples),
        grid=(blocks,),
        out_shape=jax.ShapeDtypeStruct((rows, width), jnp.bfloat16),
        in_specs=[
            pl.BlockSpec(memory_space=pltpu.SMEM),
            pl.BlockSpec(memory_space=pltpu.SMEM),
            whole((rows, width)),
            whole((rows, HEAD_DIM)),
            whole((rows, HEAD_DIM)),
            pl.BlockSpec((tok_dev, 2 * HEAD_DIM), lambda b: (b, 0)),
        ],
        out_specs=whole((rows, width)),
        scratch_shapes=[
            pltpu.VMEM((examples, 1, COLS), jnp.float32),
            pltpu.VMEM((examples, 1, COLS), jnp.float32),
            pltpu.VMEM((examples, HEAD_DIM, COLS), jnp.float32),
        ],
        compiler_params=pltpu.CompilerParams(vmem_limit_bytes=32 << 20),
        cost_estimate=pl.CostEstimate(
            flops=4 * rows * width * blocks * tok_dev,
            bytes_accessed=4 * blocks * tok_dev * HEAD_DIM,
            transcendentals=rows * GROUP * blocks * tok_dev,
        ),
    )(select, lengths, queries, test_keys, test_values, cache)


def per_device(
    queries, cache_keys, cache_values, test_keys, test_values, window_select, test_lengths, out_weight
):
    ctx_count = lax.axis_size("ctx")
    groups = lax.axis_size("kvh")
    place = lax.axis_index("ctx")
    examples_dev = queries.shape[0] // TLEN
    tok_dev = cache_keys.shape[0]
    cache = lax.all_gather(
        jnp.concatenate([cache_keys, cache_values], axis=1), "ctx", axis=0, tiled=True
    )
    lengths = lax.dynamic_slice_in_dim(test_lengths, place * examples_dev, examples_dev, 0)
    select = lax.dynamic_slice_in_dim(window_select, place * examples_dev, examples_dev, 0)
    select = jnp.repeat(select, ctx_count // WINDOWS, axis=1)
    attention = attend(queries, test_keys, test_values, cache, select, lengths, tok_dev)
    whole = lax.all_gather(attention, "ctx", axis=0, tiled=True)
    terms = jnp.dot(whole, out_weight, preferred_element_type=jnp.float32).astype(jnp.bfloat16)
    terms = terms.reshape(groups, -1, terms.shape[1])
    terms = lax.all_to_all(terms, "kvh", 0, 0, tiled=True)
    return jnp.sum(terms.astype(jnp.float32), axis=0).astype(jnp.bfloat16)


def solution(mesh):
    placed = (
        P("ctx", "kvh"),
        P("ctx", "kvh"),
        P("ctx", "kvh"),
        P("ctx", "kvh"),
        P("ctx", "kvh"),
        P(),
        P(),
        P("kvh", "ctx"),
    )
    return jax.shard_map(
        per_device, mesh=mesh, in_specs=placed, out_specs=P("kvh", "ctx"), check_vma=False
    )
```

```python
import functools
import itertools
import math

import jax
import jax.numpy as jnp
from jax import lax
from jax.experimental import pallas as pl
from jax.experimental.pallas import tpu as pltpu
from jax.sharding import Mesh
from jax.sharding import PartitionSpec as P

HEAD_DIM = 128
GROUP = 8
WINDOWS = 16
TLEN = 32
COLS = TLEN * GROUP
NEG_FILL = -1e30
SCALE = 1.0 / math.sqrt(HEAD_DIM)
LOG2E = math.log2(math.e)

SIZES = {"y": 4, "zb": 2, "za": 2, "core": 2, "zh": 2, "x": 4}
CTX = ("y", "zb", "za", "core")
KVH = ("zh", "x")
CTX_DEVICES = 32
TOP, TOTAL, STATE_ROWS = HEAD_DIM, HEAD_DIM + 1, HEAD_DIM + 8
PACKET_ROWS = HEAD_DIM + 16
VMEM_LIMIT = 48 << 20
SMEM = pl.BlockSpec(memory_space=pltpu.SMEM)
VMEM = pl.BlockSpec(memory_space=pltpu.VMEM)


def move(array, route):
    axes = tuple(route)
    places = list(itertools.product(*[range(SIZES[a]) for a in SIZES]))
    names = list(SIZES)
    pairs = set()
    index = lambda c: functools.reduce(lambda n, a: n * SIZES[a] + c[a], axes, 0)
    for place in places:
        c = dict(zip(names, place))
        pairs.add((index(c), index({a: route[a](c) for a in axes})))
    return lax.ppermute(array, axes, sorted(pairs))


def flip(array, *axes):
    return move(array, {a: (lambda c, a=a: c[a] ^ 1) for a in axes})


def from_y(array, shift):
    return move(array, {"y": lambda c: (c["y"] - shift) % SIZES["y"]})


def after(array, token):
    def kernel(array_ref, token_ref, out_ref):
        pass

    anywhere = pl.BlockSpec(memory_space=pl.ANY)
    return pl.pallas_call(
        kernel,
        out_shape=jax.ShapeDtypeStruct(array.shape, array.dtype),
        in_specs=[anywhere, anywhere],
        out_specs=anywhere,
        input_output_aliases={0: 0},
    )(array, token)


def rounded(value):
    return value.astype(jnp.bfloat16).astype(jnp.float32)


def scores(keys, columns):
    return jnp.dot(keys, columns, preferred_element_type=jnp.float32)


def soften(dots, mask=None):
    if mask is not None:
        dots = jnp.where(mask, dots, NEG_FILL)
    top = rounded(jnp.max(dots, axis=0, keepdims=True) * SCALE)
    weights = jnp.exp2(dots * (SCALE * LOG2E) - top * LOG2E)
    if mask is not None:
        weights = jnp.where(mask, weights, 0.0)
    total = rounded(jnp.sum(weights, axis=0, keepdims=True))
    return top, total, weights.astype(jnp.bfloat16)


def block_out(values_t, total, weights):
    out = jnp.dot(values_t, weights, preferred_element_type=jnp.float32)
    return rounded(out * (1.0 / jnp.maximum(total, 0.5)))


def transposed(array):
    return array.astype(jnp.float32).T.astype(jnp.bfloat16)


def absorb(blocks, seen, columns_ref, state_ref):
    examples = state_ref.shape[0]
    tiles = [(b, e) for b in range(len(blocks)) for e in range(examples)]
    values = {}

    def finish(tile, top, total, weights):
        b, e = tile
        out = block_out(values[b], total, weights)
        visible = seen(b, e)
        top = jnp.where(visible, top, NEG_FILL)
        total = jnp.where(visible, total, 0.0)
        old_top = state_ref[e, TOP : TOP + 1, :]
        joint = jnp.maximum(old_top, top)
        old = jnp.exp(old_top - joint)
        new = jnp.exp(top - joint) * total
        state_ref[e, :HEAD_DIM, :] = old * state_ref[e, :HEAD_DIM, :] + new * out
        state_ref[e, TOTAL : TOTAL + 1, :] = old * state_ref[e, TOTAL : TOTAL + 1, :] + new
        state_ref[e, TOP : TOP + 1, :] = joint

    def start(tile):
        b, e = tile
        if b not in values:
            values[b] = transposed(blocks[b][1])
        return scores(blocks[b][0], columns_ref[e])

    ahead, behind = start(tiles[0]), None
    for n, tile in enumerate(tiles):
        dots = ahead
        if n + 1 < len(tiles):
            ahead = start(tiles[n + 1])
        softened = soften(dots)
        if behind is not None:
            finish(*behind)
        behind = (tile, *softened)
    finish(*behind)


def sees(meta_ref, select_ref, own_examples, sources):
    y, zb, za, core = [meta_ref[n] for n in range(4)]
    windows = []
    for far_y, far_zb in sources:
        block = (((y + far_y) % 4 * 2 + (zb ^ far_zb)) * 2 + za) * 2 + core
        windows.append(block * WINDOWS // CTX_DEVICES)
    place = ((y * 2 + zb) * 2 + za) * 2 + core

    def seen(b, e):
        owner = place ^ (e // own_examples)
        return select_ref[owner * own_examples + e % own_examples, windows[b]] > 0

    return seen


def first_kernel(
    meta_ref, select_ref, q0_ref, q1_ref, q2_ref, q3_ref, tk_ref, tv_ref, kv_ref, columns_ref, state_ref
):
    own = q0_ref.shape[0] // TLEN
    empty = lax.broadcasted_iota(jnp.int32, (STATE_ROWS, COLS), 0) == TOP
    for r, q_ref in enumerate([q0_ref, q1_ref, q2_ref, q3_ref]):
        for e in range(own):
            rows = q_ref[e * TLEN : (e + 1) * TLEN, :]
            stacked = jnp.concatenate(
                [rows[:, h * HEAD_DIM : (h + 1) * HEAD_DIM] for h in range(GROUP)], axis=0
            )
            columns_ref[r * own + e] = transposed(stacked)
            if r > 0:
                state_ref[r * own + e] = jnp.where(empty, NEG_FILL, 0.0)
    token = lax.broadcasted_iota(jnp.int32, (TLEN, COLS), 0)
    place = lax.broadcasted_iota(jnp.int32, (TLEN, COLS), 1) % TLEN
    for e in range(own):
        rows = pl.ds(e * TLEN, TLEN)
        dots = scores(tk_ref[rows, :], columns_ref[e])
        top, total, weights = soften(dots, token <= place)
        out = block_out(transposed(tv_ref[rows, :]), total, weights)
        state_ref[e, :HEAD_DIM, :] = total * out
        state_ref[e, TOP : TOP + 1, :] = top
        state_ref[e, TOTAL : TOTAL + 1, :] = total
    seen = sees(meta_ref, select_ref, own, [(0, 0)])
    absorb([(kv_ref[0], kv_ref[1])], seen, columns_ref, state_ref)


def next_kernel(sources, last, meta_ref, select_ref, columns_ref, before_ref, *refs):
    blocks = refs[: len(sources)]
    own = before_ref.shape[0] // 4
    seen = sees(meta_ref, select_ref, own, sources)
    state_ref = refs[-1]
    state_ref[...] = before_ref[...]
    absorb([(ref[0], ref[1]) for ref in blocks], seen, columns_ref, state_ref)
    if not last:
        return
    mine_ref, near_ref, far_ref, far_near_ref = refs[len(sources) : len(sources) + 4]
    for e in range(own):
        mine_ref[e] = state_ref[e]
        near_ref[e] = state_ref[own + e]
    line = lax.broadcasted_iota(jnp.int32, (PACKET_ROWS - HEAD_DIM, COLS), 0)
    for r, packet_ref in ((2, far_ref), (3, far_near_ref)):
        for e in range(own):
            lanes = slice(e * COLS, (e + 1) * COLS)
            total = state_ref[r * own + e, TOTAL : TOTAL + 1, :]
            top = state_ref[r * own + e, TOP : TOP + 1, :]
            out = state_ref[r * own + e, :HEAD_DIM, :] * (1.0 / jnp.where(total > 0.0, total, 1.0))
            packet_ref[:HEAD_DIM, lanes] = out.astype(jnp.bfloat16)
            high = rounded(total)
            tail = jnp.where(line == 0, top, jnp.where(line == 1, high, jnp.where(line == 2, total - high, 0.0)))
            packet_ref[HEAD_DIM:, lanes] = tail.astype(jnp.bfloat16)


def finish_kernel(meta_ref, length_ref, mine_ref, near_ref, far_ref, far_near_ref, out_ref):
    own = mine_ref.shape[0]
    place = ((meta_ref[0] * 2 + meta_ref[1]) * 2 + meta_ref[2]) * 2 + meta_ref[3]
    slot = lax.broadcasted_iota(jnp.int32, (1, COLS), 1) % TLEN
    for e in range(own):
        lanes = slice(e * COLS, (e + 1) * COLS)
        parts = []
        for ref in (mine_ref, near_ref):
            parts.append((ref[e, TOP : TOP + 1, :], ref[e, TOTAL : TOTAL + 1, :], ref[e, :HEAD_DIM, :], None))
        for ref in (far_ref, far_near_ref):
            tail = ref[HEAD_DIM:, lanes].astype(jnp.float32)
            total = tail[1:2] + tail[2:3]
            parts.append((tail[0:1], total, ref[:HEAD_DIM, lanes].astype(jnp.float32), total))
        joint = functools.reduce(jnp.maximum, [part[0] for part in parts])
        over, under = 0.0, 0.0
        for top, total, out, factor in parts:
            scale = jnp.exp(top - joint)
            under = under + scale * total
            over = over + (scale if factor is None else scale * factor) * out
        live = slot < length_ref[place * own + e]
        result = jnp.where(live, over * (1.0 / under), 0.0).T
        for h in range(GROUP):
            out_ref[e * TLEN : (e + 1) * TLEN, h * HEAD_DIM : (h + 1) * HEAD_DIM] = result[
                h * TLEN : (h + 1) * TLEN, :
            ].astype(jnp.bfloat16)


def project_kernel(meta_ref, *refs):
    rows, weights = refs[:8], refs[8:12]
    keep_refs, send_refs, lined_ref, weight_ref = refs[12:14], refs[14:16], refs[16], refs[17]
    y, zb, core, zh, x = meta_ref[0], meta_ref[1], meta_ref[3], meta_ref[4], meta_ref[5]
    x1, x0 = x // 2, x % 2
    height = rows[0].shape[0]
    for k in range(4):
        weight_ref[k] = weights[k][...]
    for c in range(2):
        for s in range(4):
            row_y = (y + s) % 4
            at = (((row_y % 2) ^ x1) * 2 + ((row_y // 2) ^ zh)) * 2 + (core ^ c)
            lined_ref[pl.ds(pl.multiple_of(at * height, height), height), :] = rows[c * 4 + s][...]
    for k in range(2):
        kept, sent = ((0, 3), (1, 2)) if k == 0 else ((0, 1), (3, 2))
        for d0 in range(2):
            column = weight_ref[2 * (zb ^ x0 ^ d0) + k]
            terms = jnp.dot(lined_ref[...], column, preferred_element_type=jnp.float32)
            for d1 in range(2):
                d = 2 * d1 + d0
                part = terms[d1 * 4 * height : (d1 + 1) * 4 * height]
                if d in kept:
                    keep_refs[k][kept.index(d)] = part
                else:
                    send_refs[k][sent.index(d)] = part.astype(jnp.bfloat16)


def call(kernel, out_shape, inputs, scalars, flops=0, scratch=(), aliases={}):
    nbytes = sum(a.size * a.dtype.itemsize for a in inputs)
    many = isinstance(out_shape, (list, tuple))
    return pl.pallas_call(
        kernel,
        out_shape=out_shape,
        in_specs=[SMEM] * scalars + [VMEM] * (len(inputs) - scalars),
        out_specs=[VMEM] * len(out_shape) if many else VMEM,
        scratch_shapes=list(scratch),
        input_output_aliases=aliases,
        compiler_params=pltpu.CompilerParams(vmem_limit_bytes=VMEM_LIMIT),
        cost_estimate=pl.CostEstimate(flops=flops, bytes_accessed=nbytes, transcendentals=0),
    )(*inputs)


def per_device(
    queries, cache_keys, cache_values, test_keys, test_values, window_select, test_lengths, out_weight
):
    bf16, f32 = jnp.bfloat16, jnp.float32
    shape = jax.ShapeDtypeStruct
    rows = queries.shape[0]
    own = rows // TLEN
    tokens = cache_keys.shape[0]
    meta = jnp.stack([lax.axis_index(a) for a in SIZES]).astype(jnp.int32)
    tile_flops = 4 * COLS * tokens * HEAD_DIM * 2 * 4 * own

    cache = jnp.stack([cache_keys, cache_values])
    cache_z = flip(cache, "zb")
    cache_1, cache_3 = from_y(cache, 1), from_y(cache, 3)
    q_near = flip(queries, "core")
    q_far = flip(queries, "za")
    q_far_near = flip(q_far, "core")
    cache_2 = from_y(cache_1, 1)
    cache_z1, cache_z3 = from_y(cache_z, 1), from_y(cache_z, 3)
    cache_z2 = from_y(cache_z3, 3)
    weight = after(out_weight, cache_z)
    weights = [out_weight, flip(weight, "za"), flip(weight, "zb"), flip(weight, "zb", "za")]

    columns, state = call(
        first_kernel,
        [shape((4 * own, HEAD_DIM, COLS), bf16), shape((4 * own, STATE_ROWS, COLS), f32)],
        [meta, window_select, queries, q_near, q_far, q_far_near, test_keys, test_values, cache],
        2,
        tile_flops,
    )
    state_shape = shape(state.shape, f32)

    def absorb_blocks(state, blocks, sources):
        return call(
            functools.partial(next_kernel, sources, False),
            state_shape,
            [meta, window_select, columns, state, *blocks],
            2,
            tile_flops * len(blocks),
            aliases={3: 0},
        )

    state = absorb_blocks(state, [cache_1, cache_3], [(1, 0), (3, 0)])
    state = absorb_blocks(state, [cache_z, cache_2], [(0, 1), (2, 0)])
    state = absorb_blocks(state, [cache_z1, cache_z3], [(1, 1), (3, 1)])
    piece = shape((own, STATE_ROWS, COLS), f32)
    packet = shape((PACKET_ROWS, own * COLS), bf16)
    mine, near, far, far_near = call(
        functools.partial(next_kernel, [(2, 1)], True),
        [piece, piece, packet, packet],
        [meta, window_select, columns, state, cache_z2],
        2,
        tile_flops,
        scratch=[pltpu.VMEM(state.shape, f32)],
    )
    attention = call(
        finish_kernel,
        shape(queries.shape, bf16),
        [meta, test_lengths, mine, flip(near, "core"), flip(far, "za"), flip(far_near, "za", "core")],
        2,
    )

    rows_y = [attention] + [from_y(attention, s) for s in (1, 2, 3)]
    rows_all = rows_y + [flip(r, "core") for r in rows_y]
    width = out_weight.shape[1]
    part = (2, 4 * rows, width)
    keep_a, keep_b, send_a, send_b = call(
        project_kernel,
        [shape(part, f32), shape(part, f32), shape(part, bf16), shape(part, bf16)],
        [meta, *rows_all, *weights],
        1,
        2 * 8 * rows * out_weight.size * 4,
        scratch=[pltpu.VMEM((8 * rows, queries.shape[1]), bf16), pltpu.VMEM((4,) + out_weight.shape, bf16)],
    )
    by_1 = lambda a: move(a, {"x": lambda c: c["x"] ^ 1})
    by_3 = lambda a: move(a, {"x": lambda c: c["x"] ^ 3})
    sum_a = keep_a + by_1(send_a).astype(f32)
    sum_b = keep_b + by_3(send_b).astype(f32)
    sum_a = sum_a[0] + by_3(sum_a[1].astype(bf16)).astype(f32)
    sum_b = sum_b[0] + by_1(sum_b[1].astype(bf16)).astype(f32)
    chunks = []
    for k, total in enumerate((sum_a, sum_b)):
        halves = total.astype(bf16).reshape(2, 2 * rows, width)
        arrived = []
        for h in range(2):
            route = {
                "zb": lambda c: c["x"] % 2,
                "za": lambda c, k=k: c["za"] ^ k,
                "zh": lambda c, h=h: c["zh"] ^ h,
                "x": lambda c: c["x"] // 2 * 2 + c["zb"],
            }
            arrived.append(move(halves[h], route).astype(f32))
        chunks.append((arrived[0] + arrived[1]).astype(bf16))
    first = lax.axis_index("za") == 0
    return jnp.concatenate(
        [jnp.where(first, chunks[0], chunks[1]), jnp.where(first, chunks[1], chunks[0])], axis=0
    )


def solution(mesh):
    fine = Mesh(mesh.devices.reshape(tuple(SIZES.values())), tuple(SIZES))
    both = P(CTX, KVH)
    placed = (both, both, both, both, both, P(), P(), P(KVH, CTX))
    return jax.shard_map(
        per_device, mesh=fine, in_specs=placed, out_specs=P(KVH, CTX), check_vma=False
    )
```

```python
import functools
import itertools
import math

import jax
import jax.numpy as jnp
from jax import lax
from jax.experimental import pallas as pl
from jax.experimental.pallas import tpu as pltpu
from jax.sharding import Mesh
from jax.sharding import PartitionSpec as P

HEAD_DIM = 128
GROUP = 8
WINDOWS = 16
TLEN = 32
COLS = TLEN * GROUP
NEG_FILL = -1e30
SCALE = 1.0 / math.sqrt(HEAD_DIM)
LOG2E = math.log2(math.e)

SIZES = {"y": 4, "zb": 2, "za": 2, "core": 2, "zh": 2, "x": 4}
CTX = ("y", "zb", "za", "core")
KVH = ("zh", "x")
CTX_DEVICES = 32
TILE_FLOPS = 16
TOP, TOTAL, STATE_ROWS = HEAD_DIM, HEAD_DIM + 1, HEAD_DIM + 8
VMEM_LIMIT = 48 << 20
SMEM = pl.BlockSpec(memory_space=pltpu.SMEM)
VMEM = pl.BlockSpec(memory_space=pltpu.VMEM)
ANY = pl.BlockSpec(memory_space=pl.ANY)


def move(array, route):
    axes = tuple(route)
    places = list(itertools.product(*[range(SIZES[a]) for a in SIZES]))
    names = list(SIZES)
    pairs = set()
    index = lambda c: functools.reduce(lambda n, a: n * SIZES[a] + c[a], axes, 0)
    for place in places:
        c = dict(zip(names, place))
        pairs.add((index(c), index({a: route[a](c) for a in axes})))
    return lax.ppermute(array, axes, sorted(pairs))


def flip(array, *axes):
    return move(array, {a: (lambda c, a=a: c[a] ^ 1) for a in axes})


def from_y(array, shift):
    return move(array, {"y": lambda c: (c["y"] - shift) % SIZES["y"]})


def rounded(value):
    return value.astype(jnp.bfloat16).astype(jnp.float32)


def scores(keys, columns):
    return jnp.dot(keys, columns, preferred_element_type=jnp.float32)


def soften(dots, mask=None):
    if mask is not None:
        dots = jnp.where(mask, dots, NEG_FILL)
    top = rounded(jnp.max(dots, axis=0, keepdims=True) * SCALE)
    weights = jnp.exp2(dots * (SCALE * LOG2E) - top * LOG2E)
    if mask is not None:
        weights = jnp.where(mask, weights, 0.0)
    total = rounded(jnp.sum(weights, axis=0, keepdims=True))
    return top, total, weights.astype(jnp.bfloat16)


def block_out(values_t, total, weights):
    out = jnp.dot(values_t, weights, preferred_element_type=jnp.float32)
    return rounded(out * (1.0 / jnp.maximum(total, 0.5)))


def transposed(array):
    return array.astype(jnp.float32).T.astype(jnp.bfloat16)


def absorb(blocks, tiles, seen, columns_ref, state_ref):
    values = {}

    def finish(tile, top, total, weights):
        b, e = tile
        out = block_out(values[b], total, weights)
        visible = seen(b, e)
        top = jnp.where(visible, top, NEG_FILL)
        total = jnp.where(visible, total, 0.0)
        old_top = state_ref[e, TOP : TOP + 1, :]
        joint = jnp.maximum(old_top, top)
        old = jnp.exp(old_top - joint)
        new = jnp.exp(top - joint) * total
        state_ref[e, :HEAD_DIM, :] = old * state_ref[e, :HEAD_DIM, :] + new * out
        state_ref[e, TOTAL : TOTAL + 1, :] = old * state_ref[e, TOTAL : TOTAL + 1, :] + new
        state_ref[e, TOP : TOP + 1, :] = joint

    def start(tile):
        b, e = tile
        if b not in values:
            values[b] = transposed(blocks[b][1])
        return scores(blocks[b][0], columns_ref[e])

    ahead, behind = start(tiles[0]), None
    for n, tile in enumerate(tiles):
        dots = ahead
        if n + 1 < len(tiles):
            ahead = start(tiles[n + 1])
        softened = soften(dots)
        if behind is not None:
            finish(*behind)
        behind = (tile, *softened)
    finish(*behind)


def sees(meta_ref, select_ref, own_examples, sources):
    y, zb, za, core = [meta_ref[n] for n in range(4)]
    windows = []
    for far_y, far_zb in sources:
        block = (((y + far_y) % 4 * 2 + (zb ^ far_zb)) * 2 + za) * 2 + core
        windows.append(block * WINDOWS // CTX_DEVICES)
    place = ((y * 2 + zb) * 2 + za) * 2 + core

    def seen(b, e):
        owner = place ^ (e // own_examples)
        return select_ref[owner * own_examples + e % own_examples, windows[b]] > 0

    return seen


def make_columns(q_ref, columns_ref, first):
    for e in range(q_ref.shape[0] // TLEN):
        rows = q_ref[e * TLEN : (e + 1) * TLEN, :]
        stacked = jnp.concatenate(
            [rows[:, h * HEAD_DIM : (h + 1) * HEAD_DIM] for h in range(GROUP)], axis=0
        )
        columns_ref[first + e] = transposed(stacked)


def own_kernel(meta_ref, select_ref, q_ref, tk_ref, tv_ref, kv_ref, columns_ref, state_ref):
    own = q_ref.shape[0] // TLEN
    make_columns(q_ref, columns_ref, 0)
    token = lax.broadcasted_iota(jnp.int32, (TLEN, COLS), 0)
    place = lax.broadcasted_iota(jnp.int32, (TLEN, COLS), 1) % TLEN
    for e in range(own):
        rows = pl.ds(e * TLEN, TLEN)
        dots = scores(tk_ref[rows, :], columns_ref[e])
        top, total, weights = soften(dots, token <= place)
        out = block_out(transposed(tv_ref[rows, :]), total, weights)
        state_ref[e, :HEAD_DIM, :] = total * out
        state_ref[e, TOP : TOP + 1, :] = top
        state_ref[e, TOTAL : TOTAL + 1, :] = total
    seen = sees(meta_ref, select_ref, own, [(0, 0)])
    tiles = [(0, e) for e in range(own)]
    absorb([(kv_ref[0], kv_ref[1])], tiles, seen, columns_ref, state_ref)


def group_kernel(
    sources, meta_ref, select_ref, own_columns_ref, own_state_ref, q1_ref, q2_ref, q3_ref, *refs
):
    blocks, (columns_ref, state_ref) = refs[:-2], refs[-2:]
    own = own_state_ref.shape[0]
    columns_ref[:own] = own_columns_ref[...]
    state_ref[:own] = own_state_ref[...]
    empty = lax.broadcasted_iota(jnp.int32, (STATE_ROWS, COLS), 0) == TOP
    for r, q_ref in enumerate([q1_ref, q2_ref, q3_ref]):
        make_columns(q_ref, columns_ref, (r + 1) * own)
        for e in range(own):
            state_ref[(r + 1) * own + e] = jnp.where(empty, NEG_FILL, 0.0)
    seen = sees(meta_ref, select_ref, own, sources)
    tiles = [(b, e) for b in range(len(blocks)) for e in range(own if b == 0 else 0, 4 * own)]
    absorb([(ref[0], ref[1]) for ref in blocks], tiles, seen, columns_ref, state_ref)


def next_kernel(sources, meta_ref, select_ref, columns_ref, before_ref, *refs):
    blocks, state_ref = refs[: len(sources)], refs[-1]
    own = before_ref.shape[0] // 4
    seen = sees(meta_ref, select_ref, own, sources)
    state_ref[...] = before_ref[...]
    tiles = [(b, e) for b in range(len(blocks)) for e in range(4 * own)]
    absorb([(ref[0], ref[1]) for ref in blocks], tiles, seen, columns_ref, state_ref)


def copying_kernel(sources, meta_ref, select_ref, columns_ref, before_ref, *refs):
    blocks, (weight_ref, state_ref, copy_ref, sem) = refs[: len(sources)], refs[len(sources) :]
    copy = pltpu.make_async_copy(weight_ref, copy_ref, sem)
    copy.start()
    next_kernel(sources, meta_ref, select_ref, columns_ref, before_ref, *blocks, state_ref)
    copy.wait()


def last_kernel(sources, meta_ref, select_ref, columns_ref, before_ref, *refs):
    blocks, (mine_ref, far_ref, send_ref, state_ref) = refs[: len(sources)], refs[len(sources) :]
    next_kernel(sources, meta_ref, select_ref, columns_ref, before_ref, *blocks, state_ref)
    own = mine_ref.shape[0]
    mine_ref[...] = state_ref[:own]
    send_ref[:own] = state_ref[own : 2 * own]
    far_ref[...] = state_ref[2 * own : 3 * own]
    send_ref[own:] = state_ref[3 * own :]


def joined(parts):
    top = functools.reduce(jnp.maximum, [part[TOP : TOP + 1] for part in parts])
    total, over = 0.0, 0.0
    for part in parts:
        scale = jnp.exp(part[TOP : TOP + 1] - top)
        total = total + scale * part[TOTAL : TOTAL + 1]
        over = over + scale * part[:HEAD_DIM]
    return top, total, over


def join_kernel(far_ref, received_ref, out_ref):
    own = far_ref.shape[0]
    for e in range(own):
        top, total, over = joined([far_ref[e], received_ref[own + e]])
        out_ref[e, :HEAD_DIM, :] = over
        out_ref[e, TOP : TOP + 1, :] = top
        out_ref[e, TOTAL : TOTAL + 1, :] = total
        out_ref[e, TOTAL + 1 :, :] = jnp.zeros((STATE_ROWS - TOTAL - 1, COLS), jnp.float32)


def finish_kernel(meta_ref, length_ref, mine_ref, received_ref, far_ref, out_ref):
    own = mine_ref.shape[0]
    place = ((meta_ref[0] * 2 + meta_ref[1]) * 2 + meta_ref[2]) * 2 + meta_ref[3]
    slot = lax.broadcasted_iota(jnp.int32, (1, COLS), 1) % TLEN
    for e in range(own):
        top, total, over = joined([mine_ref[e], received_ref[e], far_ref[e]])
        live = slot < length_ref[place * own + e]
        result = jnp.where(live, over * (1.0 / total), 0.0).T
        for h in range(GROUP):
            out_ref[e * TLEN : (e + 1) * TLEN, h * HEAD_DIM : (h + 1) * HEAD_DIM] = result[
                h * TLEN : (h + 1) * TLEN, :
            ].astype(jnp.bfloat16)


def project_kernel(meta_ref, *refs):
    rows, weights = refs[:8], refs[8:13]
    keep_refs, send_refs, lined_ref, weight_ref = refs[13:15], refs[15:17], refs[17], refs[18]
    y, zb, za, core, zh, x = [meta_ref[n] for n in range(6)]
    x1, x0 = x // 2, x % 2
    height = rows[0].shape[0]
    half = weights[2].shape[0]
    weight_ref[0] = weights[0][...]
    weight_ref[1] = weights[1][...]
    weight_ref[2, :half] = weights[2][...]
    weight_ref[2, half:] = weights[3][...]
    weight_ref[3] = weights[4][...]
    for c in range(2):
        for r in range(4):
            at = (((zb ^ (r // 2)) ^ x0) * 2 + (za ^ (r % 2))) * 2 + (core ^ c)
            lined_ref[pl.ds(pl.multiple_of(at * height, height), height), :] = rows[c * 4 + r][...]
    for h in range(2):
        kept, sent = ((0, 3), (1, 2)) if h == 0 else ((0, 1), (3, 2))
        for d1 in range(2):
            column = weight_ref[(2 * (zh ^ h) + (x1 ^ d1) + 4 - y) % 4]
            terms = jnp.dot(lined_ref[...], column, preferred_element_type=jnp.float32)
            for d0 in range(2):
                d = 2 * d1 + d0
                part = terms[d0 * 4 * height : (d0 + 1) * 4 * height]
                if d in kept:
                    keep_refs[h][kept.index(d)] = part
                else:
                    send_refs[h][sent.index(d)] = part.astype(jnp.bfloat16)


def call(kernel, out_shape, inputs, scalars, flops=0, scratch=(), in_specs=None, out_specs=None):
    nbytes = sum(a.size * a.dtype.itemsize for a in inputs)
    many = isinstance(out_shape, (list, tuple))
    return pl.pallas_call(
        kernel,
        out_shape=out_shape,
        in_specs=in_specs or [SMEM] * scalars + [VMEM] * (len(inputs) - scalars),
        out_specs=out_specs or ([VMEM] * len(out_shape) if many else VMEM),
        scratch_shapes=list(scratch),
        compiler_params=pltpu.CompilerParams(vmem_limit_bytes=VMEM_LIMIT),
        cost_estimate=pl.CostEstimate(flops=flops, bytes_accessed=nbytes, transcendentals=0),
    )(*inputs)


def per_device(
    queries, cache_keys, cache_values, test_keys, test_values, window_select, test_lengths, out_weight
):
    bf16, f32 = jnp.bfloat16, jnp.float32
    shape = jax.ShapeDtypeStruct
    part = functools.partial
    rows, width = queries.shape
    own = rows // TLEN
    meta = jnp.stack([lax.axis_index(a) for a in SIZES]).astype(jnp.int32)
    scalars = [meta, window_select]
    tile_flops = TILE_FLOPS * COLS * cache_keys.shape[0] * HEAD_DIM
    columns_shape = lambda n: shape((n, HEAD_DIM, COLS), bf16)
    state_shape = lambda n: shape((n, STATE_ROWS, COLS), f32)

    cache = jnp.stack([cache_keys, cache_values])
    cache_z = flip(cache, "zb")
    cache_1, cache_3 = from_y(cache, 1), from_y(cache, 3)
    q_far = flip(queries, "za")
    q_near = flip(queries, "core")
    q_far_near = flip(q_far, "core")
    cache_2 = from_y(cache_1, 1)
    cache_z1, cache_z3 = from_y(cache_z, 1), from_y(cache_z, 3)
    cache_z2 = from_y(cache_z3, 3)

    own_columns, own_state = call(
        own_kernel,
        [columns_shape(own), state_shape(own)],
        scalars + [queries, test_keys, test_values, cache],
        2,
        2 * own * tile_flops,
    )
    columns, state = call(
        part(group_kernel, [(0, 0), (1, 0), (3, 0)]),
        [columns_shape(4 * own), state_shape(4 * own)],
        scalars + [own_columns, own_state, q_near, q_far, q_far_near, cache, cache_1, cache_3],
        2,
        11 * own * tile_flops,
    )
    state, weight = call(
        part(copying_kernel, [(0, 1), (2, 0)]),
        [state_shape(4 * own), shape(out_weight.shape, bf16)],
        scalars + [columns, state, cache_z, cache_2, out_weight],
        2,
        8 * own * tile_flops,
        scratch=[pltpu.SemaphoreType.DMA],
        in_specs=[SMEM] * 2 + [VMEM] * 4 + [ANY],
        out_specs=[VMEM, ANY],
    )
    state = call(
        part(next_kernel, [(1, 1), (3, 1)]),
        state_shape(4 * own),
        scalars + [columns, state, cache_z1, cache_z3],
        2,
        8 * own * tile_flops,
    )
    mine, far, send = call(
        part(last_kernel, [(2, 1)]),
        [state_shape(own), state_shape(own), state_shape(2 * own)],
        scalars + [columns, state, cache_z2],
        2,
        4 * own * tile_flops,
        scratch=[pltpu.VMEM(state.shape, f32)],
    )
    received = flip(send, "core")
    joined_far = call(join_kernel, state_shape(own), [far, received], 0)
    attention = call(
        finish_kernel,
        shape(queries.shape, bf16),
        [meta, test_lengths, mine, received, flip(joined_far, "za")],
        2,
    )

    half = out_weight.shape[0] // 2
    weight_1, weight_3 = from_y(weight, 1), from_y(weight, 3)
    weights = [out_weight, weight_1, from_y(weight_3[:half], 3), from_y(weight_1[half:], 1), weight_3]

    rows_z = [attention, flip(attention, "za"), flip(attention, "zb"), flip(attention, "zb", "za")]
    rows_all = rows_z + [flip(r, "core") for r in rows_z]
    terms = lambda dtype: shape((2, 4 * rows, out_weight.shape[1]), dtype)
    keep_a, keep_b, send_a, send_b = call(
        project_kernel,
        [terms(f32), terms(f32), terms(bf16), terms(bf16)],
        [meta, *rows_all, *weights],
        1,
        2 * 8 * rows * out_weight.size * 4,
        scratch=[pltpu.VMEM((8 * rows, width), bf16), pltpu.VMEM((4,) + out_weight.shape, bf16)],
    )
    by_1 = lambda a: move(a, {"x": lambda c: c["x"] ^ 1})
    by_3 = lambda a: move(a, {"x": lambda c: c["x"] ^ 3})
    sum_a = keep_a + by_1(send_a).astype(f32)
    sum_b = keep_b + by_3(send_b).astype(f32)
    sum_a = sum_a[0] + by_3(sum_a[1])
    sum_b = sum_b[0] + by_1(sum_b[1])
    arrived = []
    for h, total in enumerate((sum_a, sum_b)):
        route = {
            "y": lambda c, h=h: 2 * (c["zh"] ^ h) + c["x"] // 2,
            "zh": lambda c: c["y"] // 2,
            "x": lambda c: c["y"] % 2 * 2 + c["x"] % 2,
        }
        arrived.append(move(total.astype(bf16), route).astype(f32))
    return (arrived[0] + arrived[1]).astype(bf16)


def solution(mesh):
    fine = Mesh(mesh.devices.reshape(tuple(SIZES.values())), tuple(SIZES))
    both = P(CTX, KVH)
    placed = (both, both, both, both, both, P(), P(), P(KVH, CTX))
    return jax.shard_map(
        per_device, mesh=fine, in_specs=placed, out_specs=P(KVH, CTX), check_vma=False
    )
```

```python
import functools
import itertools
import math

import jax
import jax.numpy as jnp
from jax import lax
from jax.experimental import pallas as pl
from jax.experimental.pallas import tpu as pltpu
from jax.sharding import Mesh
from jax.sharding import PartitionSpec as P

HEAD_DIM = 128
GROUP = 8
WINDOWS = 16
TLEN = 32
COLS = TLEN * GROUP
NEG_FILL = -1e30
SCALE = 1.0 / math.sqrt(HEAD_DIM)
LOG2E = math.log2(math.e)

SIZES = {"y": 4, "zb": 2, "za": 2, "core": 2, "zh": 2, "x": 4}
CTX = ("y", "zb", "za", "core")
KVH = ("zh", "x")
CTX_DEVICES = 32
TILE_FLOPS = 16
TOP, TOTAL, STATE_ROWS = HEAD_DIM, HEAD_DIM + 1, HEAD_DIM + 8
VMEM_LIMIT = 48 << 20
SMEM = pl.BlockSpec(memory_space=pltpu.SMEM)
VMEM = pl.BlockSpec(memory_space=pltpu.VMEM)


def move(array, route):
    axes = tuple(route)
    places = list(itertools.product(*[range(SIZES[a]) for a in SIZES]))
    names = list(SIZES)
    pairs = set()
    index = lambda c: functools.reduce(lambda n, a: n * SIZES[a] + c[a], axes, 0)
    for place in places:
        c = dict(zip(names, place))
        pairs.add((index(c), index({a: route[a](c) for a in axes})))
    return lax.ppermute(array, axes, sorted(pairs))


def flip(array, *axes):
    return move(array, {a: (lambda c, a=a: c[a] ^ 1) for a in axes})


def from_y(array, shift):
    return move(array, {"y": lambda c: (c["y"] - shift) % SIZES["y"]})


def rounded(value):
    return value.astype(jnp.bfloat16).astype(jnp.float32)


def scores(keys, columns):
    return jnp.dot(keys, columns, preferred_element_type=jnp.float32)


def soften(dots, mask=None):
    if mask is not None:
        dots = jnp.where(mask, dots, NEG_FILL)
    top = rounded(jnp.max(dots, axis=0, keepdims=True) * SCALE)
    weights = jnp.exp2(dots * (SCALE * LOG2E) - top * LOG2E)
    if mask is not None:
        weights = jnp.where(mask, weights, 0.0)
    total = rounded(jnp.sum(weights, axis=0, keepdims=True))
    return top, total, weights.astype(jnp.bfloat16)


def block_out(values_t, total, weights):
    out = jnp.dot(values_t, weights, preferred_element_type=jnp.float32)
    return rounded(out * (1.0 / jnp.maximum(total, 0.5)))


def transposed(array):
    return array.astype(jnp.float32).T.astype(jnp.bfloat16)


def absorb(blocks, tiles, seen, columns_ref, state_ref):
    values = {}

    def finish(tile, top, total, weights):
        b, e = tile
        out = block_out(values[b], total, weights)
        visible = seen(b, e)
        top = jnp.where(visible, top, NEG_FILL)
        total = jnp.where(visible, total, 0.0)
        old_top = state_ref[e, TOP : TOP + 1, :]
        joint = jnp.maximum(old_top, top)
        old = jnp.exp(old_top - joint)
        new = jnp.exp(top - joint) * total
        state_ref[e, :HEAD_DIM, :] = old * state_ref[e, :HEAD_DIM, :] + new * out
        state_ref[e, TOTAL : TOTAL + 1, :] = old * state_ref[e, TOTAL : TOTAL + 1, :] + new
        state_ref[e, TOP : TOP + 1, :] = joint

    def start(tile):
        b, e = tile
        if b not in values:
            values[b] = transposed(blocks[b][1])
        return scores(blocks[b][0], columns_ref[e])

    ahead, behind = start(tiles[0]), None
    for n, tile in enumerate(tiles):
        dots = ahead
        if n + 1 < len(tiles):
            ahead = start(tiles[n + 1])
        softened = soften(dots)
        if behind is not None:
            finish(*behind)
        behind = (tile, *softened)
    finish(*behind)


def sees(meta_ref, select_ref, own_examples, sources):
    y, zb, za, core = [meta_ref[n] for n in range(4)]
    windows = []
    for far_y, far_zb in sources:
        block = (((y + far_y) % 4 * 2 + (zb ^ far_zb)) * 2 + za) * 2 + core
        windows.append(block * WINDOWS // CTX_DEVICES)
    place = ((y * 2 + zb) * 2 + za) * 2 + core

    def seen(b, e):
        owner = place ^ (e // own_examples)
        return select_ref[owner * own_examples + e % own_examples, windows[b]] > 0

    return seen


def make_columns(q_ref, columns_ref, first):
    for e in range(q_ref.shape[0] // TLEN):
        rows = q_ref[e * TLEN : (e + 1) * TLEN, :]
        stacked = jnp.concatenate(
            [rows[:, h * HEAD_DIM : (h + 1) * HEAD_DIM] for h in range(GROUP)], axis=0
        )
        columns_ref[first + e] = transposed(stacked)


def own_kernel(meta_ref, select_ref, q_ref, test_ref, kv_ref, columns_ref, state_ref):
    own = q_ref.shape[0] // TLEN
    make_columns(q_ref, columns_ref, 0)
    token = lax.broadcasted_iota(jnp.int32, (TLEN, COLS), 0)
    place = lax.broadcasted_iota(jnp.int32, (TLEN, COLS), 1) % TLEN
    for e in range(own):
        rows = pl.ds(e * TLEN, TLEN)
        dots = scores(test_ref[rows, :HEAD_DIM], columns_ref[e])
        top, total, weights = soften(dots, token <= place)
        out = block_out(transposed(test_ref[rows, HEAD_DIM:]), total, weights)
        state_ref[e, :HEAD_DIM, :] = total * out
        state_ref[e, TOP : TOP + 1, :] = top
        state_ref[e, TOTAL : TOTAL + 1, :] = total
    seen = sees(meta_ref, select_ref, own, [(0, 0)])
    tiles = [(0, e) for e in range(own)]
    absorb([(kv_ref[0], kv_ref[1])], tiles, seen, columns_ref, state_ref)


def group_kernel(
    sources, meta_ref, select_ref, own_columns_ref, own_state_ref, q1_ref, q2_ref, q3_ref, *refs
):
    blocks, (columns_ref, state_ref) = refs[:-2], refs[-2:]
    own = own_state_ref.shape[0]
    columns_ref[:own] = own_columns_ref[...]
    state_ref[:own] = own_state_ref[...]
    empty = lax.broadcasted_iota(jnp.int32, (STATE_ROWS, COLS), 0) == TOP
    for r, q_ref in enumerate([q1_ref, q2_ref, q3_ref]):
        make_columns(q_ref, columns_ref, (r + 1) * own)
        for e in range(own):
            state_ref[(r + 1) * own + e] = jnp.where(empty, NEG_FILL, 0.0)
    seen = sees(meta_ref, select_ref, own, sources)
    tiles = [(b, e) for b in range(len(blocks)) for e in range(own if b == 0 else 0, 4 * own)]
    absorb([(ref[0], ref[1]) for ref in blocks], tiles, seen, columns_ref, state_ref)


def next_kernel(sources, meta_ref, select_ref, columns_ref, before_ref, *refs):
    blocks, state_ref = refs[: len(sources)], refs[-1]
    own = before_ref.shape[0] // 4
    seen = sees(meta_ref, select_ref, own, sources)
    state_ref[...] = before_ref[...]
    tiles = [(b, e) for b in range(len(blocks)) for e in range(4 * own)]
    absorb([(ref[0], ref[1]) for ref in blocks], tiles, seen, columns_ref, state_ref)


def last_kernel(sources, meta_ref, select_ref, columns_ref, before_ref, *refs):
    blocks, (mine_ref, far_ref, send_ref, state_ref) = refs[: len(sources)], refs[len(sources) :]
    next_kernel(sources, meta_ref, select_ref, columns_ref, before_ref, *blocks, state_ref)
    own = mine_ref.shape[0]
    mine_ref[...] = state_ref[:own]
    send_ref[:own] = state_ref[own : 2 * own]
    far_ref[...] = state_ref[2 * own : 3 * own]
    send_ref[own:] = state_ref[3 * own :]


def joined(parts):
    top = functools.reduce(jnp.maximum, [part[TOP : TOP + 1] for part in parts])
    total, over = 0.0, 0.0
    for part in parts:
        scale = jnp.exp(part[TOP : TOP + 1] - top)
        total = total + scale * part[TOTAL : TOTAL + 1]
        over = over + scale * part[:HEAD_DIM]
    return top, total, over


def join_kernel(far_ref, received_ref, out_ref):
    own = far_ref.shape[0]
    for e in range(own):
        top, total, over = joined([far_ref[e], received_ref[own + e]])
        out_ref[e, :HEAD_DIM, :] = over
        out_ref[e, TOP : TOP + 1, :] = top
        out_ref[e, TOTAL : TOTAL + 1, :] = total
        out_ref[e, TOTAL + 1 :, :] = jnp.zeros((STATE_ROWS - TOTAL - 1, COLS), jnp.float32)


def finish_kernel(meta_ref, length_ref, mine_ref, received_ref, far_ref, token_ref, out_ref):
    own = mine_ref.shape[0]
    place = ((meta_ref[0] * 2 + meta_ref[1]) * 2 + meta_ref[2]) * 2 + meta_ref[3]
    slot = lax.broadcasted_iota(jnp.int32, (1, COLS), 1) % TLEN
    for e in range(own):
        top, total, over = joined([mine_ref[e], received_ref[e], far_ref[e]])
        live = slot < length_ref[place * own + e]
        result = jnp.where(live, over * (1.0 / total), 0.0).T
        for h in range(GROUP):
            out_ref[e * TLEN : (e + 1) * TLEN, h * HEAD_DIM : (h + 1) * HEAD_DIM] = result[
                h * TLEN : (h + 1) * TLEN, :
            ].astype(jnp.bfloat16)


def project_kernel(meta_ref, *refs):
    rows, weight_ref = refs[:8], refs[8]
    keep_refs, send_refs, lined_ref = refs[9:11], refs[11:13], refs[13]
    y, za, core, zh, x = [meta_ref[n] for n in (0, 2, 3, 4, 5)]
    x1, x0 = x // 2, x % 2
    height = rows[0].shape[0]
    for c in range(2):
        for s in range(4):
            row_y = (y + s) % 4
            at = (((row_y % 2) ^ x1) * 2 + ((row_y // 2) ^ zh)) * 2 + (core ^ c)
            lined_ref[pl.ds(pl.multiple_of(at * height, height), height), :] = rows[c * 4 + s][...]
    for k in range(2):
        kept, sent = ((0, 3), (1, 2)) if k == 0 else ((0, 1), (3, 2))
        for d0 in range(2):
            column = weight_ref[2 * (x0 ^ d0) + (za ^ k)]
            terms = jnp.dot(lined_ref[...], column, preferred_element_type=jnp.float32)
            for d1 in range(2):
                d = 2 * d1 + d0
                part = terms[d1 * 4 * height : (d1 + 1) * 4 * height]
                if d in kept:
                    keep_refs[k][kept.index(d)] = part
                else:
                    send_refs[k][sent.index(d)] = part.astype(jnp.bfloat16)


def call(kernel, out_shape, inputs, scalars, flops=0, scratch=()):
    nbytes = sum(a.size * a.dtype.itemsize for a in inputs)
    many = isinstance(out_shape, (list, tuple))
    return pl.pallas_call(
        kernel,
        out_shape=out_shape,
        in_specs=[SMEM] * scalars + [VMEM] * (len(inputs) - scalars),
        out_specs=[VMEM] * len(out_shape) if many else VMEM,
        scratch_shapes=list(scratch),
        compiler_params=pltpu.CompilerParams(vmem_limit_bytes=VMEM_LIMIT),
        cost_estimate=pl.CostEstimate(flops=flops, bytes_accessed=nbytes, transcendentals=0),
    )(*inputs)


def per_device(
    queries, cache_keys, cache_values, test_keys, test_values, window_select, test_lengths, out_weight
):
    bf16, f32 = jnp.bfloat16, jnp.float32
    shape = jax.ShapeDtypeStruct
    part = functools.partial
    rows, width = queries.shape
    own = rows // TLEN
    meta = jnp.stack([lax.axis_index(a) for a in SIZES]).astype(jnp.int32)
    scalars = [meta, window_select]
    tile_flops = TILE_FLOPS * COLS * cache_keys.shape[0] * HEAD_DIM
    columns_shape = lambda n: shape((n, HEAD_DIM, COLS), bf16)
    state_shape = lambda n: shape((n, STATE_ROWS, COLS), f32)

    weight = lax.all_gather(out_weight, ("zb", "za"), axis=0)

    cache = jnp.stack([cache_keys, cache_values])
    cache_z = flip(cache, "zb")
    cache_1, cache_3, cache_2 = from_y(cache, 1), from_y(cache, 3), from_y(cache, 2)
    q_far = flip(queries, "za")
    q_near = flip(queries, "core")
    q_far_near = flip(q_far, "core")
    cache_z1, cache_z3, cache_z2 = from_y(cache_z, 1), from_y(cache_z, 3), from_y(cache_z, 2)

    own_columns, own_state = call(
        own_kernel,
        [columns_shape(own), state_shape(own)],
        scalars + [queries, jnp.concatenate([test_keys, test_values], axis=1), cache],
        2,
        2 * own * tile_flops,
    )
    columns, state = call(
        part(group_kernel, [(0, 0), (1, 0), (3, 0)]),
        [columns_shape(4 * own), state_shape(4 * own)],
        scalars + [own_columns, own_state, q_near, q_far, q_far_near, cache, cache_1, cache_3],
        2,
        11 * own * tile_flops,
    )
    state = call(
        part(next_kernel, [(0, 1), (2, 0)]),
        state_shape(4 * own),
        scalars + [columns, state, cache_z, cache_2],
        2,
        8 * own * tile_flops,
    )
    mine, far, send = call(
        part(last_kernel, [(1, 1), (3, 1), (2, 1)]),
        [state_shape(own), state_shape(own), state_shape(2 * own)],
        scalars + [columns, state, cache_z1, cache_z3, cache_z2],
        2,
        12 * own * tile_flops,
        scratch=[pltpu.VMEM(state.shape, f32)],
    )
    received = flip(send, "core")
    joined_far = call(join_kernel, state_shape(own), [far, received], 0)
    attention = call(
        finish_kernel,
        shape(queries.shape, bf16),
        [meta, test_lengths, mine, received, flip(joined_far, "za"), weight[0, :16, :HEAD_DIM]],
        2,
    )

    rows_y = [attention] + [from_y(attention, s) for s in (1, 2, 3)]
    rows_all = rows_y + [flip(r, "core") for r in rows_y]
    terms = lambda dtype: shape((2, 4 * rows, out_weight.shape[1]), dtype)
    keep_a, keep_b, send_a, send_b = call(
        project_kernel,
        [terms(f32), terms(f32), terms(bf16), terms(bf16)],
        [meta, *rows_all, weight],
        1,
        2 * 8 * rows * out_weight.size * 4,
        scratch=[pltpu.VMEM((8 * rows, width), bf16)],
    )
    by_1 = lambda a: move(a, {"x": lambda c: c["x"] ^ 1})
    by_3 = lambda a: move(a, {"x": lambda c: c["x"] ^ 3})
    sum_a = keep_a + by_1(send_a).astype(f32)
    sum_b = keep_b + by_3(send_b).astype(f32)
    sum_a = sum_a[0] + by_3(sum_a[1])
    sum_b = sum_b[0] + by_1(sum_b[1])
    chunks = []
    for k, total in enumerate((sum_a, sum_b)):
        arrived = []
        for h in range(2):
            route = {
                "zb": lambda c: c["x"] % 2,
                "za": lambda c, k=k: c["za"] ^ k,
                "zh": lambda c, h=h: c["zh"] ^ h,
                "x": lambda c: c["x"] // 2 * 2 + c["zb"],
            }
            piece = total[h * 2 * rows : (h + 1) * 2 * rows]
            arrived.append(move(piece if h == 0 else piece.astype(bf16), route).astype(f32))
        chunks.append((arrived[0] + arrived[1]).astype(bf16))
    first = lax.axis_index("za") == 0
    return jnp.concatenate(
        [jnp.where(first, chunks[0], chunks[1]), jnp.where(first, chunks[1], chunks[0])], axis=0
    )


def solution(mesh):
    fine = Mesh(mesh.devices.reshape(tuple(SIZES.values())), tuple(SIZES))
    both = P(CTX, KVH)
    placed = (both, both, both, both, both, P(), P(), P(KVH, CTX))
    return jax.shard_map(
        per_device, mesh=fine, in_specs=placed, out_specs=P(KVH, CTX), check_vma=False
    )
```

```python
import functools
import itertools
import math

import jax
import jax.numpy as jnp
from jax import lax
from jax.experimental import pallas as pl
from jax.experimental.pallas import tpu as pltpu
from jax.sharding import Mesh
from jax.sharding import PartitionSpec as P

HEAD_DIM = 128
GROUP = 8
WINDOWS = 16
TLEN = 32
COLS = TLEN * GROUP
NEG_FILL = -1e30
SCALE = 1.0 / math.sqrt(HEAD_DIM)
LOG2E = math.log2(math.e)

SIZES = {"y": 4, "zb": 2, "za": 2, "core": 2, "zh": 2, "x": 4}
CTX = ("y", "zb", "za", "core")
KVH = ("zh", "x")
CTX_DEVICES = 32
TILE_FLOPS = 16
TOP, TOTAL, STATE_ROWS = HEAD_DIM, HEAD_DIM + 1, HEAD_DIM + 8
VMEM_LIMIT = 48 << 20
SMEM = pl.BlockSpec(memory_space=pltpu.SMEM)
VMEM = pl.BlockSpec(memory_space=pltpu.VMEM)


def move(array, route):
    axes = tuple(route)
    places = list(itertools.product(*[range(SIZES[a]) for a in SIZES]))
    names = list(SIZES)
    pairs = set()
    index = lambda c: functools.reduce(lambda n, a: n * SIZES[a] + c[a], axes, 0)
    for place in places:
        c = dict(zip(names, place))
        pairs.add((index(c), index({a: route[a](c) for a in axes})))
    return lax.ppermute(array, axes, sorted(pairs))


def flip(array, *axes):
    return move(array, {a: (lambda c, a=a: c[a] ^ 1) for a in axes})


def from_y(array, shift):
    return move(array, {"y": lambda c: (c["y"] - shift) % SIZES["y"]})


def rounded(value):
    return value.astype(jnp.bfloat16).astype(jnp.float32)


def scores(keys, columns):
    return jnp.dot(keys, columns, preferred_element_type=jnp.float32)


def soften(dots, mask=None):
    if mask is not None:
        dots = jnp.where(mask, dots, NEG_FILL)
    top = rounded(jnp.max(dots, axis=0, keepdims=True) * SCALE)
    weights = jnp.exp2(dots * (SCALE * LOG2E) - top * LOG2E)
    if mask is not None:
        weights = jnp.where(mask, weights, 0.0)
    total = rounded(jnp.sum(weights, axis=0, keepdims=True))
    return top, total, weights.astype(jnp.bfloat16)


def block_out(values_t, total, weights):
    out = jnp.dot(values_t, weights, preferred_element_type=jnp.float32)
    return rounded(out * (1.0 / jnp.maximum(total, 0.5)))


def transposed(array):
    return array.astype(jnp.float32).T.astype(jnp.bfloat16)


def absorb(blocks, tiles, seen, columns, states):
    values = {}

    def finish(tile, top, total, weights):
        b, r, e = tile
        out = block_out(values[b], total, weights)
        visible = seen(b, r, e)
        top = jnp.where(visible, top, NEG_FILL)
        total = jnp.where(visible, total, 0.0)
        state_ref = states[r]
        old_top = state_ref[e, TOP : TOP + 1, :]
        joint = jnp.maximum(old_top, top)
        old = jnp.exp(old_top - joint)
        new = jnp.exp(top - joint) * total
        state_ref[e, :HEAD_DIM, :] = old * state_ref[e, :HEAD_DIM, :] + new * out
        state_ref[e, TOTAL : TOTAL + 1, :] = old * state_ref[e, TOTAL : TOTAL + 1, :] + new
        state_ref[e, TOP : TOP + 1, :] = joint

    def start(tile):
        b, r, e = tile
        if b not in values:
            values[b] = transposed(blocks[b][1])
        return scores(blocks[b][0], columns[r][e])

    ahead, behind = start(tiles[0]), None
    for n, tile in enumerate(tiles):
        dots = ahead
        if n + 1 < len(tiles):
            ahead = start(tiles[n + 1])
        softened = soften(dots)
        if behind is not None:
            finish(*behind)
        behind = (tile, *softened)
    finish(*behind)


def sees(meta_ref, select_ref, own_examples, sources):
    y, zb, za, core = [meta_ref[n] for n in range(4)]
    windows = []
    for far_y, far_zb in sources:
        block = (((y + far_y) % 4 * 2 + (zb ^ far_zb)) * 2 + za) * 2 + core
        windows.append(block * WINDOWS // CTX_DEVICES)
    place = ((y * 2 + zb) * 2 + za) * 2 + core

    def seen(b, r, e):
        return select_ref[(place ^ r) * own_examples + e, windows[b]] > 0

    return seen


def make_columns(q_ref, columns_ref):
    for e in range(q_ref.shape[0] // TLEN):
        rows = q_ref[e * TLEN : (e + 1) * TLEN, :]
        stacked = jnp.concatenate(
            [rows[:, h * HEAD_DIM : (h + 1) * HEAD_DIM] for h in range(GROUP)], axis=0
        )
        columns_ref[e] = transposed(stacked)


def own_kernel(meta_ref, select_ref, q_ref, test_ref, kv_ref, columns_ref, state_ref):
    own = q_ref.shape[0] // TLEN
    make_columns(q_ref, columns_ref)
    token = lax.broadcasted_iota(jnp.int32, (TLEN, COLS), 0)
    place = lax.broadcasted_iota(jnp.int32, (TLEN, COLS), 1) % TLEN
    for e in range(own):
        rows = pl.ds(e * TLEN, TLEN)
        dots = scores(test_ref[rows, :HEAD_DIM], columns_ref[e])
        top, total, weights = soften(dots, token <= place)
        out = block_out(transposed(test_ref[rows, HEAD_DIM:]), total, weights)
        state_ref[e, :HEAD_DIM, :] = total * out
        state_ref[e, TOP : TOP + 1, :] = top
        state_ref[e, TOTAL : TOTAL + 1, :] = total
    seen = sees(meta_ref, select_ref, own, [(0, 0)])
    tiles = [(0, 0, e) for e in range(own)]
    absorb([(kv_ref[0], kv_ref[1])], tiles, seen, [columns_ref], [state_ref])


def group_kernel(sources, meta_ref, select_ref, own_columns_ref, own_state_ref, *refs):
    queries, blocks = refs[:3], refs[3 : 3 + len(sources)]
    others, states = refs[3 + len(sources) : 6 + len(sources)], refs[6 + len(sources) :]
    own = own_state_ref.shape[0]
    states[0][...] = own_state_ref[...]
    empty = lax.broadcasted_iota(jnp.int32, (STATE_ROWS, COLS), 0) == TOP
    for r in range(3):
        make_columns(queries[r], others[r])
        for e in range(own):
            states[r + 1][e] = jnp.where(empty, NEG_FILL, 0.0)
    seen = sees(meta_ref, select_ref, own, sources)
    tiles = [(b, r, e) for b in range(len(blocks)) for r in range(b == 0, 4) for e in range(own)]
    pairs = [(ref[0], ref[1]) for ref in blocks]
    absorb(pairs, tiles, seen, [own_columns_ref, *others], states)


def next_kernel(sources, members, meta_ref, select_ref, *refs):
    columns, before, refs = refs[:2], refs[2:4], refs[4:]
    blocks, states = refs[: len(sources)], refs[len(sources) :][-2:]
    own = before[0].shape[0]
    for n in range(2):
        states[n][...] = before[n][...]
    seen = sees(meta_ref, select_ref, own, sources)
    tiles = [(b, n, e) for b in range(len(blocks)) for n in range(2) for e in range(own)]
    pairs = [(ref[0], ref[1]) for ref in blocks]
    absorb(pairs, tiles, lambda b, n, e: seen(b, members[n], e), columns, states)


def joined(parts):
    top = functools.reduce(jnp.maximum, [part[TOP : TOP + 1] for part in parts])
    total, over = 0.0, 0.0
    for part in parts:
        scale = jnp.exp(part[TOP : TOP + 1] - top)
        total = total + scale * part[TOTAL : TOTAL + 1]
        over = over + scale * part[:HEAD_DIM]
    return top, total, over


def join_kernel(far_ref, received_ref, out_ref):
    own = far_ref.shape[0]
    for e in range(own):
        top, total, over = joined([far_ref[e], received_ref[e]])
        out_ref[e, :HEAD_DIM, :] = over
        out_ref[e, TOP : TOP + 1, :] = top
        out_ref[e, TOTAL : TOTAL + 1, :] = total
        out_ref[e, TOTAL + 1 :, :] = jnp.zeros((STATE_ROWS - TOTAL - 1, COLS), jnp.float32)


def finish_kernel(meta_ref, length_ref, mine_ref, received_ref, far_ref, *tokens_and_out):
    out_ref = tokens_and_out[-1]
    own = mine_ref.shape[0]
    place = ((meta_ref[0] * 2 + meta_ref[1]) * 2 + meta_ref[2]) * 2 + meta_ref[3]
    slot = lax.broadcasted_iota(jnp.int32, (1, COLS), 1) % TLEN
    for e in range(own):
        top, total, over = joined([mine_ref[e], received_ref[e], far_ref[e]])
        live = slot < length_ref[place * own + e]
        result = jnp.where(live, over * (1.0 / total), 0.0).T
        for h in range(GROUP):
            out_ref[e * TLEN : (e + 1) * TLEN, h * HEAD_DIM : (h + 1) * HEAD_DIM] = result[
                h * TLEN : (h + 1) * TLEN, :
            ].astype(jnp.bfloat16)


def project_kernel(meta_ref, *refs):
    rows, weights = refs[:8], refs[8:14]
    keep_refs, send_refs, lined_ref, weight_ref = refs[14:16], refs[16:18], refs[18], refs[19]
    y, zb, za, core, zh, x = [meta_ref[n] for n in range(6)]
    height = rows[0].shape[0]
    half = weights[1].shape[0]
    weight_ref[0] = weights[0][...]
    weight_ref[1, :half], weight_ref[1, half:] = weights[1][...], weights[2][...]
    weight_ref[2] = weights[3][...]
    weight_ref[3, :half], weight_ref[3, half:] = weights[4][...], weights[5][...]
    for c in range(2):
        for r in range(4):
            at = (((y // 2) ^ (r // 2) ^ zh) * 2 + (za ^ (r % 2))) * 2 + (core ^ c)
            lined_ref[pl.ds(pl.multiple_of(at * height, height), height), :] = rows[c * 4 + r][...]
    for d in range(4):
        column = weight_ref[2 * ((y % 2) ^ (x // 2) ^ (d // 2)) + (zb ^ (x % 2) ^ (d % 2))]
        terms = jnp.dot(lined_ref[...], column, preferred_element_type=jnp.float32)
        for h in range(2):
            kept, sent = ((0, 3), (1, 2)) if h == 0 else ((0, 1), (3, 2))
            part = terms[h * 4 * height : (h + 1) * 4 * height]
            if d in kept:
                keep_refs[h][kept.index(d)] = part
            else:
                send_refs[h][sent.index(d)] = part.astype(jnp.bfloat16)


def call(kernel, out_shape, inputs, scalars, flops=0, scratch=()):
    nbytes = sum(a.size * a.dtype.itemsize for a in inputs)
    many = isinstance(out_shape, (list, tuple))
    return pl.pallas_call(
        kernel,
        out_shape=out_shape,
        in_specs=[SMEM] * scalars + [VMEM] * (len(inputs) - scalars),
        out_specs=[VMEM] * len(out_shape) if many else VMEM,
        scratch_shapes=list(scratch),
        compiler_params=pltpu.CompilerParams(vmem_limit_bytes=VMEM_LIMIT),
        cost_estimate=pl.CostEstimate(flops=flops, bytes_accessed=nbytes, transcendentals=0),
    )(*inputs)


def per_device(
    queries, cache_keys, cache_values, test_keys, test_values, window_select, test_lengths, out_weight
):
    bf16, f32 = jnp.bfloat16, jnp.float32
    shape = jax.ShapeDtypeStruct
    part = functools.partial
    rows, width = queries.shape
    own = rows // TLEN
    meta = jnp.stack([lax.axis_index(a) for a in SIZES]).astype(jnp.int32)
    scalars = [meta, window_select]
    tile_flops = TILE_FLOPS * COLS * cache_keys.shape[0] * HEAD_DIM
    columns_shape = lambda n: shape((n, HEAD_DIM, COLS), bf16)
    state_shape = lambda n: shape((n, STATE_ROWS, COLS), f32)

    cache = jnp.stack([cache_keys, cache_values])
    cache_z = flip(cache, "zb")
    cache_1, cache_3, cache_2 = from_y(cache, 1), from_y(cache, 3), from_y(cache, 2)
    q_far = flip(queries, "za")
    q_near = flip(queries, "core")
    q_far_near = flip(q_far, "core")
    cache_z1, cache_z3, cache_z2 = from_y(cache_z, 1), from_y(cache_z, 3), from_y(cache_z, 2)

    own_columns, own_state = call(
        own_kernel,
        [columns_shape(own), state_shape(own)],
        scalars + [queries, jnp.concatenate([test_keys, test_values], axis=1), cache],
        2,
        2 * own * tile_flops,
    )
    def next_blocks(states, members, blocks, sources, token=()):
        before = [states[r] for r in members]
        after = call(
            part(next_kernel, sources, members),
            [state_shape(own)] * 2,
            scalars + [columns[r] for r in members] + before + blocks + list(token),
            2,
            2 * len(blocks) * own * tile_flops,
        )
        for n, r in enumerate(members):
            states[r] = after[n]

    outputs = call(
        part(group_kernel, [(0, 0), (1, 0), (3, 0)]),
        [columns_shape(own)] * 3 + [state_shape(own)] * 4,
        scalars + [own_columns, own_state, q_near, q_far, q_far_near, cache, cache_1, cache_3],
        2,
        11 * own * tile_flops,
    )
    columns, states = [own_columns, *outputs[:3]], list(outputs[3:])
    near_z, far_z = [cache_z, cache_2], [cache_z1, cache_z3, cache_z2]
    near_places, far_places = [(0, 1), (2, 0)], [(1, 1), (3, 1), (2, 1)]
    half = out_weight.shape[0] // 2
    weight_za = flip(out_weight[:half], "zb")
    weight_zb = flip(out_weight[half:], "zb")
    y_1 = lambda a: move(a, {"y": lambda c: c["y"] ^ 1})
    weight_y = y_1(out_weight)
    next_blocks(states, (2, 3), near_z, near_places)
    next_blocks(states, (2, 3), far_z, far_places, [weight_za])
    received_far = flip(states[3], "core")
    next_blocks(states, (0, 1), near_z, near_places)
    joined_far = call(join_kernel, state_shape(own), [states[2], received_far], 0)
    received_far = flip(joined_far, "za")
    next_blocks(states, (0, 1), far_z[:2], far_places[:2], [joined_far])
    next_blocks(states, (0, 1), far_z[2:], far_places[2:], [received_far, weight_zb, weight_y])
    received = flip(states[1], "core")
    attention = call(
        finish_kernel,
        shape(queries.shape, bf16),
        [meta, test_lengths, states[0], received, received_far] + [],
        2,
    )

    weights = [out_weight, weight_za, weight_zb, weight_y, y_1(weight_za), y_1(weight_zb)]

    y_3 = lambda c: c["y"] ^ 3
    rows_y = [attention, flip(attention, "za"), move(attention, {"y": y_3})]
    rows_y.append(move(attention, {"y": y_3, "za": lambda c: c["za"] ^ 1}))
    rows_all = rows_y + [flip(r, "core") for r in rows_y]
    terms = lambda dtype: shape((2, 4 * rows, out_weight.shape[1]), dtype)
    keep_a, keep_b, send_a, send_b = call(
        project_kernel,
        [terms(f32), terms(f32), terms(bf16), terms(bf16)],
        [meta, *rows_all, *weights],
        1,
        2 * 8 * rows * out_weight.size * 4,
        scratch=[pltpu.VMEM((8 * rows, width), bf16), pltpu.VMEM((4,) + out_weight.shape, bf16)],
    )
    by_1 = lambda a: move(a, {"x": lambda c: c["x"] ^ 1})
    by_3 = lambda a: move(a, {"x": lambda c: c["x"] ^ 3})
    sum_a = keep_a + by_1(send_a).astype(f32)
    sum_b = keep_b + by_3(send_b).astype(f32)
    sum_a = sum_a[0] + by_3(sum_a[1])
    sum_b = sum_b[0] + by_1(sum_b[1])
    arrived = []
    for h, total in enumerate((sum_a, sum_b.astype(bf16))):
        route = {
            "y": lambda c: c["y"] // 2 * 2 + c["x"] // 2,
            "zb": lambda c: c["x"] % 2,
            "zh": lambda c, h=h: c["zh"] ^ h,
            "x": lambda c, h=h: 2 * ((c["y"] % 2) ^ (c["y"] // 2) ^ c["zh"] ^ h) + c["zb"],
        }
        arrived.append(move(total, route).astype(f32))
    return (arrived[0] + arrived[1]).astype(bf16)


def solution(mesh):
    fine = Mesh(mesh.devices.reshape(tuple(SIZES.values())), tuple(SIZES))
    both = P(CTX, KVH)
    placed = (both, both, both, both, both, P(), P(), P(KVH, CTX))
    return jax.shard_map(
        per_device, mesh=fine, in_specs=placed, out_specs=P(KVH, CTX), check_vma=False
    )
```

```python
import functools
import itertools
import math

import jax
import jax.numpy as jnp
from jax import lax
from jax.experimental import pallas as pl
from jax.experimental.pallas import tpu as pltpu
from jax.sharding import Mesh
from jax.sharding import PartitionSpec as P

HEAD_DIM = 128
GROUP = 8
WINDOWS = 16
TLEN = 32
COLS = TLEN * GROUP
NEG_FILL = -1e30
SCALE = 1.0 / math.sqrt(HEAD_DIM)
LOG2E = math.log2(math.e)

SIZES = {"y": 4, "zb": 2, "za": 2, "core": 2, "zh": 2, "x": 4}
CTX = ("y", "zb", "za", "core")
KVH = ("zh", "x")
CTX_DEVICES = 32
TILE_FLOPS = 16
TOP, TOTAL, STATE_ROWS = HEAD_DIM, HEAD_DIM + 1, HEAD_DIM + 8
VMEM_LIMIT = 48 << 20
SMEM = pl.BlockSpec(memory_space=pltpu.SMEM)
VMEM = pl.BlockSpec(memory_space=pltpu.VMEM)
ANY = pl.BlockSpec(memory_space=pl.ANY)


def move(array, route):
    axes = tuple(route)
    places = list(itertools.product(*[range(SIZES[a]) for a in SIZES]))
    names = list(SIZES)
    pairs = set()
    index = lambda c: functools.reduce(lambda n, a: n * SIZES[a] + c[a], axes, 0)
    for place in places:
        c = dict(zip(names, place))
        pairs.add((index(c), index({a: route[a](c) for a in axes})))
    return lax.ppermute(array, axes, sorted(pairs))


def flip(array, *axes):
    return move(array, {a: (lambda c, a=a: c[a] ^ 1) for a in axes})


def from_y(array, shift):
    return move(array, {"y": lambda c: (c["y"] - shift) % SIZES["y"]})


def rounded(value):
    return value.astype(jnp.bfloat16).astype(jnp.float32)


def scores(keys, columns):
    return jnp.dot(keys, columns, preferred_element_type=jnp.float32)


def soften(dots, mask=None):
    if mask is not None:
        dots = jnp.where(mask, dots, NEG_FILL)
    top = rounded(jnp.max(dots, axis=0, keepdims=True) * SCALE)
    weights = jnp.exp2(dots * (SCALE * LOG2E) - top * LOG2E)
    if mask is not None:
        weights = jnp.where(mask, weights, 0.0)
    total = rounded(jnp.sum(weights, axis=0, keepdims=True))
    return top, total, weights.astype(jnp.bfloat16)


def block_out(values_t, total, weights):
    out = jnp.dot(values_t, weights, preferred_element_type=jnp.float32)
    return rounded(out * (1.0 / jnp.maximum(total, 0.5)))


def transposed(array):
    return array.astype(jnp.float32).T.astype(jnp.bfloat16)


def absorb(blocks, tiles, seen, columns, states):
    values = {}

    def finish(tile, top, total, weights):
        b, r, e = tile
        out = block_out(values[b], total, weights)
        visible = seen(b, r, e)
        top = jnp.where(visible, top, NEG_FILL)
        total = jnp.where(visible, total, 0.0)
        state_ref = states[r]
        old_top = state_ref[e, TOP : TOP + 1, :]
        joint = jnp.maximum(old_top, top)
        old = jnp.exp(old_top - joint)
        new = jnp.exp(top - joint) * total
        state_ref[e, :HEAD_DIM, :] = old * state_ref[e, :HEAD_DIM, :] + new * out
        state_ref[e, TOTAL : TOTAL + 1, :] = old * state_ref[e, TOTAL : TOTAL + 1, :] + new
        state_ref[e, TOP : TOP + 1, :] = joint

    def start(tile):
        b, r, e = tile
        if b not in values:
            values[b] = transposed(blocks[b][1])
        return scores(blocks[b][0], columns[r][e])

    ahead, behind = start(tiles[0]), None
    for n, tile in enumerate(tiles):
        dots = ahead
        if n + 1 < len(tiles):
            ahead = start(tiles[n + 1])
        softened = soften(dots)
        if behind is not None:
            finish(*behind)
        behind = (tile, *softened)
    finish(*behind)


def sees(meta_ref, select_ref, own_examples, sources):
    y, zb, za, core = [meta_ref[n] for n in range(4)]
    windows = []
    for far_y, far_zb in sources:
        block = (((y + far_y) % 4 * 2 + (zb ^ far_zb)) * 2 + za) * 2 + core
        windows.append(block * WINDOWS // CTX_DEVICES)
    place = ((y * 2 + zb) * 2 + za) * 2 + core

    def seen(b, r, e):
        return select_ref[(place ^ r) * own_examples + e, windows[b]] > 0

    return seen


def make_columns(q_ref, columns_ref):
    for e in range(q_ref.shape[0] // TLEN):
        rows = q_ref[e * TLEN : (e + 1) * TLEN, :]
        stacked = jnp.concatenate(
            [rows[:, h * HEAD_DIM : (h + 1) * HEAD_DIM] for h in range(GROUP)], axis=0
        )
        columns_ref[e] = transposed(stacked)


def own_kernel(
    meta_ref, select_ref, q_ref, test_ref, kv_ref, weight_ref, columns_ref, state_ref, copy_ref, sem
):
    copy = pltpu.make_async_copy(weight_ref, copy_ref, sem)
    copy.start()
    own = q_ref.shape[0] // TLEN
    make_columns(q_ref, columns_ref)
    token = lax.broadcasted_iota(jnp.int32, (TLEN, COLS), 0)
    place = lax.broadcasted_iota(jnp.int32, (TLEN, COLS), 1) % TLEN
    for e in range(own):
        rows = pl.ds(e * TLEN, TLEN)
        dots = scores(test_ref[rows, :HEAD_DIM], columns_ref[e])
        top, total, weights = soften(dots, token <= place)
        out = block_out(transposed(test_ref[rows, HEAD_DIM:]), total, weights)
        state_ref[e, :HEAD_DIM, :] = total * out
        state_ref[e, TOP : TOP + 1, :] = top
        state_ref[e, TOTAL : TOTAL + 1, :] = total
    seen = sees(meta_ref, select_ref, own, [(0, 0)])
    tiles = [(0, 0, e) for e in range(own)]
    absorb([(kv_ref[0], kv_ref[1])], tiles, seen, [columns_ref], [state_ref])
    copy.wait()


def group_kernel(sources, meta_ref, select_ref, own_columns_ref, own_state_ref, *refs):
    queries, blocks = refs[:3], refs[3 : 3 + len(sources)]
    others, states = refs[3 + len(sources) : 6 + len(sources)], refs[6 + len(sources) :]
    own = own_state_ref.shape[0]
    states[0][...] = own_state_ref[...]
    empty = lax.broadcasted_iota(jnp.int32, (STATE_ROWS, COLS), 0) == TOP
    for r in range(3):
        make_columns(queries[r], others[r])
        for e in range(own):
            states[r + 1][e] = jnp.where(empty, NEG_FILL, 0.0)
    seen = sees(meta_ref, select_ref, own, sources)
    tiles = [(b, r, e) for b in range(len(blocks)) for r in range(b == 0, 4) for e in range(own)]
    pairs = [(ref[0], ref[1]) for ref in blocks]
    absorb(pairs, tiles, seen, [own_columns_ref, *others], states)


def next_kernel(sources, members, meta_ref, select_ref, *refs):
    columns, before, refs = refs[:2], refs[2:4], refs[4:]
    blocks, states = refs[: len(sources)], refs[len(sources) :][-2:]
    own = before[0].shape[0]
    for n in range(2):
        states[n][...] = before[n][...]
    seen = sees(meta_ref, select_ref, own, sources)
    tiles = [(b, n, e) for b in range(len(blocks)) for n in range(2) for e in range(own)]
    pairs = [(ref[0], ref[1]) for ref in blocks]
    absorb(pairs, tiles, lambda b, n, e: seen(b, members[n], e), columns, states)


def joined(parts):
    top = functools.reduce(jnp.maximum, [part[TOP : TOP + 1] for part in parts])
    total, over = 0.0, 0.0
    for part in parts:
        scale = jnp.exp(part[TOP : TOP + 1] - top)
        total = total + scale * part[TOTAL : TOTAL + 1]
        over = over + scale * part[:HEAD_DIM]
    return top, total, over


def join_kernel(far_ref, received_ref, out_ref):
    own = far_ref.shape[0]
    for e in range(own):
        top, total, over = joined([far_ref[e], received_ref[e]])
        out_ref[e, :HEAD_DIM, :] = over
        out_ref[e, TOP : TOP + 1, :] = top
        out_ref[e, TOTAL : TOTAL + 1, :] = total
        out_ref[e, TOTAL + 1 :, :] = jnp.zeros((STATE_ROWS - TOTAL - 1, COLS), jnp.float32)


def finish_kernel(meta_ref, length_ref, mine_ref, received_ref, far_ref, *tokens_and_out):
    out_ref = tokens_and_out[-1]
    own = mine_ref.shape[0]
    place = ((meta_ref[0] * 2 + meta_ref[1]) * 2 + meta_ref[2]) * 2 + meta_ref[3]
    slot = lax.broadcasted_iota(jnp.int32, (1, COLS), 1) % TLEN
    for e in range(own):
        top, total, over = joined([mine_ref[e], received_ref[e], far_ref[e]])
        live = slot < length_ref[place * own + e]
        result = jnp.where(live, over * (1.0 / total), 0.0).T
        for h in range(GROUP):
            out_ref[e * TLEN : (e + 1) * TLEN, h * HEAD_DIM : (h + 1) * HEAD_DIM] = result[
                h * TLEN : (h + 1) * TLEN, :
            ].astype(jnp.bfloat16)


def project_kernel(meta_ref, *refs):
    rows, weights = refs[:8], refs[8:14]
    keep_refs, send_refs, lined_ref, weight_ref = refs[14:16], refs[16:18], refs[18], refs[19]
    y, zb, core, zh, x = [meta_ref[n] for n in (0, 1, 3, 4, 5)]
    x1, x0 = x // 2, x % 2
    height = rows[0].shape[0]
    half = weights[2].shape[0]
    weight_ref[0], weight_ref[1] = weights[0][...], weights[1][...]
    for n in (2, 3):
        weight_ref[n, :half], weight_ref[n, half:] = weights[2 * n - 2][...], weights[2 * n - 1][...]
    for c in range(2):
        for s in range(4):
            row_y = (y + s) % 4
            at = (((row_y % 2) ^ x1) * 2 + ((row_y // 2) ^ zh)) * 2 + (core ^ c)
            lined_ref[pl.ds(pl.multiple_of(at * height, height), height), :] = rows[c * 4 + s][...]
    for k in range(2):
        kept, sent = ((0, 3), (1, 2)) if k == 0 else ((0, 1), (3, 2))
        for d0 in range(2):
            column = weight_ref[2 * (zb ^ x0 ^ d0) + k]
            terms = jnp.dot(lined_ref[...], column, preferred_element_type=jnp.float32)
            for d1 in range(2):
                d = 2 * d1 + d0
                part = terms[d1 * 4 * height : (d1 + 1) * 4 * height]
                if d in kept:
                    keep_refs[k][kept.index(d)] = part
                else:
                    send_refs[k][sent.index(d)] = part.astype(jnp.bfloat16)


def call(kernel, out_shape, inputs, scalars, flops=0, scratch=(), anywhere=0):
    nbytes = sum(a.size * a.dtype.itemsize for a in inputs)
    many = isinstance(out_shape, (list, tuple))
    return pl.pallas_call(
        kernel,
        out_shape=out_shape,
        in_specs=[SMEM] * scalars + [VMEM] * (len(inputs) - scalars - anywhere) + [ANY] * anywhere,
        out_specs=[VMEM] * (len(out_shape) - anywhere) + [ANY] * anywhere if many else VMEM,
        scratch_shapes=list(scratch),
        compiler_params=pltpu.CompilerParams(vmem_limit_bytes=VMEM_LIMIT),
        cost_estimate=pl.CostEstimate(flops=flops, bytes_accessed=nbytes, transcendentals=0),
    )(*inputs)


def per_device(
    queries, cache_keys, cache_values, test_keys, test_values, window_select, test_lengths, out_weight
):
    bf16, f32 = jnp.bfloat16, jnp.float32
    shape = jax.ShapeDtypeStruct
    part = functools.partial
    rows, width = queries.shape
    own = rows // TLEN
    meta = jnp.stack([lax.axis_index(a) for a in SIZES]).astype(jnp.int32)
    scalars = [meta, window_select]
    tile_flops = TILE_FLOPS * COLS * cache_keys.shape[0] * HEAD_DIM
    columns_shape = lambda n: shape((n, HEAD_DIM, COLS), bf16)
    state_shape = lambda n: shape((n, STATE_ROWS, COLS), f32)

    cache = jnp.stack([cache_keys, cache_values])
    cache_z = flip(cache, "zb")
    cache_1, cache_3 = from_y(cache, 1), from_y(cache, 3)
    cache_2 = from_y(cache_1, 1)
    q_far = flip(queries, "za")
    q_near = flip(queries, "core")
    q_far_near = flip(q_far, "core")
    cache_z1, cache_z3, cache_z2 = from_y(cache_z, 1), from_y(cache_z, 3), from_y(cache_z, 2)

    own_columns, own_state, weight = call(
        own_kernel,
        [columns_shape(own), state_shape(own), shape(out_weight.shape, bf16)],
        scalars
        + [queries, jnp.concatenate([test_keys, test_values], axis=1), cache, out_weight],
        2,
        2 * own * tile_flops,
        scratch=[pltpu.SemaphoreType.DMA],
        anywhere=1,
    )

    def next_blocks(states, members, blocks, sources, token=()):
        before = [states[r] for r in members]
        after = call(
            part(next_kernel, sources, members),
            [state_shape(own)] * 2,
            scalars + [columns[r] for r in members] + before + blocks + list(token),
            2,
            2 * len(blocks) * own * tile_flops,
        )
        for n, r in enumerate(members):
            states[r] = after[n]

    outputs = call(
        part(group_kernel, [(0, 0), (1, 0), (3, 0)]),
        [columns_shape(own)] * 3 + [state_shape(own)] * 4,
        scalars + [own_columns, own_state, q_near, q_far, q_far_near, cache, cache_1, cache_3],
        2,
        11 * own * tile_flops,
    )
    columns, states = [own_columns, *outputs[:3]], list(outputs[3:])
    near_z, far_z = [cache_z, cache_2], [cache_z1, cache_z3, cache_z2]
    near_places, far_places = [(0, 1), (2, 0)], [(1, 1), (3, 1), (2, 1)]
    half = out_weight.shape[0] // 2
    weight_a = flip(weight, "za")
    weight_z = [flip(weight[:half], "zb"), flip(weight[half:], "zb")]
    next_blocks(states, (2, 3), near_z, near_places)
    next_blocks(states, (2, 3), far_z, far_places, [weight_z[0], weight_a])
    received_far = flip(states[3], "core")
    next_blocks(states, (0, 1), near_z, near_places)
    joined_far = call(join_kernel, state_shape(own), [states[2], received_far], 0)
    received_far = flip(joined_far, "za")
    next_blocks(states, (0, 1), far_z[:2], far_places[:2], [joined_far])
    next_blocks(states, (0, 1), far_z[2:], far_places[2:], [received_far, weight_z[1]])
    received = flip(states[1], "core")
    attention = call(
        finish_kernel,
        shape(queries.shape, bf16),
        [meta, test_lengths, states[0], received, received_far] + [],
        2,
    )

    weights = [out_weight, weight_a, *weight_z, *[flip(w, "za") for w in weight_z]]

    rows_y = [attention] + [from_y(attention, s) for s in (1, 2, 3)]
    rows_all = rows_y + [flip(r, "core") for r in rows_y]
    terms = lambda dtype: shape((2, 4 * rows, out_weight.shape[1]), dtype)
    keep_a, keep_b, send_a, send_b = call(
        project_kernel,
        [terms(f32), terms(f32), terms(bf16), terms(bf16)],
        [meta, *rows_all, *weights],
        1,
        2 * 8 * rows * out_weight.size * 4,
        scratch=[pltpu.VMEM((8 * rows, width), bf16), pltpu.VMEM((4,) + out_weight.shape, bf16)],
    )
    by_1 = lambda a: move(a, {"x": lambda c: c["x"] ^ 1})
    by_3 = lambda a: move(a, {"x": lambda c: c["x"] ^ 3})
    sum_a = keep_a + by_1(send_a).astype(f32)
    sum_b = keep_b + by_3(send_b).astype(f32)
    sum_a = sum_a[0] + by_3(sum_a[1])
    sum_b = sum_b[0] + by_1(sum_b[1])
    chunks = []
    for k, total in enumerate((sum_a, sum_b)):
        arrived = []
        for h in range(2):
            route = {
                "zb": lambda c: c["x"] % 2,
                "za": lambda c, k=k: c["za"] ^ k,
                "zh": lambda c, h=h: c["zh"] ^ h,
                "x": lambda c: c["x"] // 2 * 2 + c["zb"],
            }
            piece = total[h * 2 * rows : (h + 1) * 2 * rows]
            arrived.append(move(piece if h == 0 else piece.astype(bf16), route).astype(f32))
        chunks.append((arrived[0] + arrived[1]).astype(bf16))
    first = lax.axis_index("za") == 0
    return jnp.concatenate(
        [jnp.where(first, chunks[0], chunks[1]), jnp.where(first, chunks[1], chunks[0])], axis=0
    )


def solution(mesh):
    fine = Mesh(mesh.devices.reshape(tuple(SIZES.values())), tuple(SIZES))
    both = P(CTX, KVH)
    placed = (both, both, both, both, both, P(), P(), P(KVH, CTX))
    return jax.shard_map(
        per_device, mesh=fine, in_specs=placed, out_specs=P(KVH, CTX), check_vma=False
    )
```

```python
import functools
import itertools
import math

import jax
import jax.numpy as jnp
from jax import lax
from jax.experimental import pallas as pl
from jax.experimental.pallas import tpu as pltpu
from jax.sharding import Mesh
from jax.sharding import PartitionSpec as P

HEAD_DIM = 128
GROUP = 8
WINDOWS = 16
TLEN = 32
COLS = TLEN * GROUP
NEG_FILL = -1e30
SCALE = 1.0 / math.sqrt(HEAD_DIM)
LOG2E = math.log2(math.e)

SIZES = {"y": 4, "zb": 2, "za": 2, "core": 2, "zh": 2, "x": 4}
CTX = ("y", "zb", "za", "core")
KVH = ("zh", "x")
CTX_DEVICES = 32
TILE_FLOPS = 16
TOP, TOTAL, STATE_ROWS = HEAD_DIM, HEAD_DIM + 1, HEAD_DIM + 8
VMEM_LIMIT = 48 << 20
SMEM = pl.BlockSpec(memory_space=pltpu.SMEM)
VMEM = pl.BlockSpec(memory_space=pltpu.VMEM)
ANY = pl.BlockSpec(memory_space=pl.ANY)


def move(array, route):
    axes = tuple(route)
    places = list(itertools.product(*[range(SIZES[a]) for a in SIZES]))
    names = list(SIZES)
    pairs = set()
    index = lambda c: functools.reduce(lambda n, a: n * SIZES[a] + c[a], axes, 0)
    for place in places:
        c = dict(zip(names, place))
        pairs.add((index(c), index({a: route[a](c) for a in axes})))
    return lax.ppermute(array, axes, sorted(pairs))


def flip(array, *axes):
    return move(array, {a: (lambda c, a=a: c[a] ^ 1) for a in axes})


def from_y(array, shift):
    return move(array, {"y": lambda c: (c["y"] - shift) % SIZES["y"]})


def after(array, token):
    def kernel(array_ref, token_ref, out_ref):
        pass

    return pl.pallas_call(
        kernel,
        out_shape=jax.ShapeDtypeStruct(array.shape, array.dtype),
        in_specs=[ANY, ANY],
        out_specs=ANY,
        input_output_aliases={0: 0},
    )(array, token)


def rounded(value):
    return value.astype(jnp.bfloat16).astype(jnp.float32)


def scores(keys, columns):
    return jnp.dot(keys, columns, preferred_element_type=jnp.float32)


def soften(dots, mask=None):
    if mask is not None:
        dots = jnp.where(mask, dots, NEG_FILL)
    top = rounded(jnp.max(dots, axis=0, keepdims=True) * SCALE)
    weights = jnp.exp2(dots * (SCALE * LOG2E) - top * LOG2E)
    if mask is not None:
        weights = jnp.where(mask, weights, 0.0)
    total = rounded(jnp.sum(weights, axis=0, keepdims=True))
    return top, total, weights.astype(jnp.bfloat16)


def block_out(values_t, total, weights):
    out = jnp.dot(values_t, weights, preferred_element_type=jnp.float32)
    return rounded(out * (1.0 / jnp.maximum(total, 0.5)))


def transposed(array):
    return array.astype(jnp.float32).T.astype(jnp.bfloat16)


def absorb(blocks, tiles, seen, columns, states):
    values = {}

    def finish(tile, top, total, weights):
        b, r, e = tile
        out = block_out(values[b], total, weights)
        visible = seen(b, r, e)
        top = jnp.where(visible, top, NEG_FILL)
        total = jnp.where(visible, total, 0.0)
        state_ref = states[r]
        old_top = state_ref[e, TOP : TOP + 1, :]
        joint = jnp.maximum(old_top, top)
        old = jnp.exp(old_top - joint)
        new = jnp.exp(top - joint) * total
        state_ref[e, :HEAD_DIM, :] = old * state_ref[e, :HEAD_DIM, :] + new * out
        state_ref[e, TOTAL : TOTAL + 1, :] = old * state_ref[e, TOTAL : TOTAL + 1, :] + new
        state_ref[e, TOP : TOP + 1, :] = joint

    def start(tile):
        b, r, e = tile
        if b not in values:
            values[b] = transposed(blocks[b][1])
        return scores(blocks[b][0], columns[r][e])

    ahead, behind = start(tiles[0]), None
    for n, tile in enumerate(tiles):
        dots = ahead
        if n + 1 < len(tiles):
            ahead = start(tiles[n + 1])
        softened = soften(dots)
        if behind is not None:
            finish(*behind)
        behind = (tile, *softened)
    finish(*behind)


def sees(meta_ref, select_ref, own_examples, sources):
    y, zb, za, core = [meta_ref[n] for n in range(4)]
    windows = []
    for far_y, far_zb in sources:
        block = (((y + far_y) % 4 * 2 + (zb ^ far_zb)) * 2 + za) * 2 + core
        windows.append(block * WINDOWS // CTX_DEVICES)
    place = ((y * 2 + zb) * 2 + za) * 2 + core

    def seen(b, r, e):
        return select_ref[(place ^ r) * own_examples + e, windows[b]] > 0

    return seen


def make_columns(q_ref, columns_ref):
    for e in range(q_ref.shape[0] // TLEN):
        rows = q_ref[e * TLEN : (e + 1) * TLEN, :]
        stacked = jnp.concatenate(
            [rows[:, h * HEAD_DIM : (h + 1) * HEAD_DIM] for h in range(GROUP)], axis=0
        )
        columns_ref[e] = transposed(stacked)


def own_kernel(meta_ref, select_ref, q_ref, test_ref, kv_ref, columns_ref, state_ref):
    own = q_ref.shape[0] // TLEN
    make_columns(q_ref, columns_ref)
    token = lax.broadcasted_iota(jnp.int32, (TLEN, COLS), 0)
    place = lax.broadcasted_iota(jnp.int32, (TLEN, COLS), 1) % TLEN
    for e in range(own):
        rows = pl.ds(e * TLEN, TLEN)
        dots = scores(test_ref[rows, :HEAD_DIM], columns_ref[e])
        top, total, weights = soften(dots, token <= place)
        out = block_out(transposed(test_ref[rows, HEAD_DIM:]), total, weights)
        state_ref[e, :HEAD_DIM, :] = total * out
        state_ref[e, TOP : TOP + 1, :] = top
        state_ref[e, TOTAL : TOTAL + 1, :] = total
    seen = sees(meta_ref, select_ref, own, [(0, 0)])
    tiles = [(0, 0, e) for e in range(own)]
    absorb([(kv_ref[0], kv_ref[1])], tiles, seen, [columns_ref], [state_ref])


def group_kernel(sources, meta_ref, select_ref, own_columns_ref, own_state_ref, *refs):
    queries, blocks, refs = refs[:3], refs[3 : 3 + len(sources)], refs[3 + len(sources) :]
    weight_ref, others, states, copy_ref, sem = refs[0], refs[1:4], refs[4:8], refs[8], refs[9]
    copy = pltpu.make_async_copy(weight_ref, copy_ref, sem)
    copy.start()
    own = own_state_ref.shape[0]
    states[0][...] = own_state_ref[...]
    empty = lax.broadcasted_iota(jnp.int32, (STATE_ROWS, COLS), 0) == TOP
    for r in range(3):
        make_columns(queries[r], others[r])
        for e in range(own):
            states[r + 1][e] = jnp.where(empty, NEG_FILL, 0.0)
    seen = sees(meta_ref, select_ref, own, sources)
    tiles = [(b, r, e) for b in range(len(blocks)) for r in range(b == 0, 4) for e in range(own)]
    pairs = [(ref[0], ref[1]) for ref in blocks]
    absorb(pairs, tiles, seen, [own_columns_ref, *others], states)
    copy.wait()


def next_kernel(sources, meta_ref, select_ref, *refs):
    columns, before, blocks, states = refs[:4], refs[4:8], refs[8 : 8 + len(sources)], refs[-4:]
    own = before[0].shape[0]
    for r in range(4):
        states[r][...] = before[r][...]
    seen = sees(meta_ref, select_ref, own, sources)
    tiles = [(b, r, e) for b in range(len(blocks)) for r in range(4) for e in range(own)]
    absorb([(ref[0], ref[1]) for ref in blocks], tiles, seen, columns, states)


def joined(parts):
    top = functools.reduce(jnp.maximum, [part[TOP : TOP + 1] for part in parts])
    total, over = 0.0, 0.0
    for part in parts:
        scale = jnp.exp(part[TOP : TOP + 1] - top)
        total = total + scale * part[TOTAL : TOTAL + 1]
        over = over + scale * part[:HEAD_DIM]
    return top, total, over


def join_kernel(far_ref, received_ref, out_ref):
    own = far_ref.shape[0]
    for e in range(own):
        top, total, over = joined([far_ref[e], received_ref[e]])
        out_ref[e, :HEAD_DIM, :] = over
        out_ref[e, TOP : TOP + 1, :] = top
        out_ref[e, TOTAL : TOTAL + 1, :] = total
        out_ref[e, TOTAL + 1 :, :] = jnp.zeros((STATE_ROWS - TOTAL - 1, COLS), jnp.float32)


def finish_kernel(meta_ref, length_ref, mine_ref, received_ref, far_ref, *tokens_and_out):
    out_ref = tokens_and_out[-1]
    own = mine_ref.shape[0]
    place = ((meta_ref[0] * 2 + meta_ref[1]) * 2 + meta_ref[2]) * 2 + meta_ref[3]
    slot = lax.broadcasted_iota(jnp.int32, (1, COLS), 1) % TLEN
    for e in range(own):
        top, total, over = joined([mine_ref[e], received_ref[e], far_ref[e]])
        live = slot < length_ref[place * own + e]
        result = jnp.where(live, over * (1.0 / total), 0.0).T
        for h in range(GROUP):
            out_ref[e * TLEN : (e + 1) * TLEN, h * HEAD_DIM : (h + 1) * HEAD_DIM] = result[
                h * TLEN : (h + 1) * TLEN, :
            ].astype(jnp.bfloat16)


def project_kernel(meta_ref, *refs):
    rows, weights = refs[:8], refs[8:14]
    keep_refs, send_refs, lined_ref, weight_ref = refs[14:16], refs[16:18], refs[18], refs[19]
    y, zb, core, zh, x = [meta_ref[n] for n in (0, 1, 3, 4, 5)]
    x1, x0 = x // 2, x % 2
    height = rows[0].shape[0]
    half = weights[2].shape[0]
    weight_ref[0], weight_ref[1] = weights[0][...], weights[1][...]
    for n in (2, 3):
        weight_ref[n, :half], weight_ref[n, half:] = weights[2 * n - 2][...], weights[2 * n - 1][...]
    for c in range(2):
        for s in range(4):
            row_y = (y + s) % 4
            at = (((row_y % 2) ^ x1) * 2 + ((row_y // 2) ^ zh)) * 2 + (core ^ c)
            lined_ref[pl.ds(pl.multiple_of(at * height, height), height), :] = rows[c * 4 + s][...]
    for k in range(2):
        kept, sent = ((0, 3), (1, 2)) if k == 0 else ((0, 1), (3, 2))
        for d0 in range(2):
            column = weight_ref[2 * (zb ^ x0 ^ d0) + k]
            terms = jnp.dot(lined_ref[...], column, preferred_element_type=jnp.float32)
            for d1 in range(2):
                d = 2 * d1 + d0
                part = terms[d1 * 4 * height : (d1 + 1) * 4 * height]
                if d in kept:
                    keep_refs[k][kept.index(d)] = part
                else:
                    send_refs[k][sent.index(d)] = part.astype(jnp.bfloat16)


def call(kernel, out_shape, inputs, scalars, flops=0, scratch=(), anywhere=0):
    nbytes = sum(a.size * a.dtype.itemsize for a in inputs)
    many = isinstance(out_shape, (list, tuple))
    return pl.pallas_call(
        kernel,
        out_shape=out_shape,
        in_specs=[SMEM] * scalars + [VMEM] * (len(inputs) - scalars - anywhere) + [ANY] * anywhere,
        out_specs=[VMEM] * (len(out_shape) - anywhere) + [ANY] * anywhere if many else VMEM,
        scratch_shapes=list(scratch),
        compiler_params=pltpu.CompilerParams(vmem_limit_bytes=VMEM_LIMIT),
        cost_estimate=pl.CostEstimate(flops=flops, bytes_accessed=nbytes, transcendentals=0),
    )(*inputs)


def per_device(
    queries, cache_keys, cache_values, test_keys, test_values, window_select, test_lengths, out_weight
):
    bf16, f32 = jnp.bfloat16, jnp.float32
    shape = jax.ShapeDtypeStruct
    part = functools.partial
    rows, width = queries.shape
    own = rows // TLEN
    meta = jnp.stack([lax.axis_index(a) for a in SIZES]).astype(jnp.int32)
    scalars = [meta, window_select]
    tile_flops = TILE_FLOPS * COLS * cache_keys.shape[0] * HEAD_DIM
    columns_shape = lambda n: shape((n, HEAD_DIM, COLS), bf16)
    state_shape = lambda n: shape((n, STATE_ROWS, COLS), f32)

    cache = jnp.stack([cache_keys, cache_values])
    cache_z = flip(cache, "zb")
    cache_1, cache_3 = from_y(cache, 1), from_y(cache, 3)
    cache_2 = from_y(cache_1, 1)
    q_far = flip(queries, "za")
    q_near = flip(queries, "core")
    q_far_near = flip(q_far, "core")
    cache_z1, cache_z3 = from_y(cache_z, 1), from_y(cache_z, 3)
    cache_z2 = from_y(cache_z3, 3)

    own_columns, own_state = call(
        own_kernel,
        [columns_shape(own), state_shape(own)],
        scalars + [queries, jnp.concatenate([test_keys, test_values], axis=1), cache],
        2,
        2 * own * tile_flops,
    )
    outputs = call(
        part(group_kernel, [(0, 0), (1, 0), (3, 0)]),
        [columns_shape(own)] * 3 + [state_shape(own)] * 4 + [shape(out_weight.shape, bf16)],
        scalars + [own_columns, own_state, q_near, q_far, q_far_near, cache, cache_1, cache_3, out_weight],
        2,
        11 * own * tile_flops,
        scratch=[pltpu.SemaphoreType.DMA],
        anywhere=1,
    )
    columns, states, weight = [own_columns, *outputs[:3]], outputs[3:7], outputs[7]
    half = out_weight.shape[0] // 2
    weight_a = flip(weight, "za")
    weight_z = [flip(weight[:half], "zb"), flip(weight[half:], "zb")]

    def next_blocks(states, blocks, sources, tokens=()):
        return call(
            part(next_kernel, sources),
            [state_shape(own)] * 4,
            scalars + [*columns, *states, *blocks, *tokens],
            2,
            4 * len(blocks) * own * tile_flops,
        )

    states = next_blocks(states, [cache_z, cache_2], [(0, 1), (2, 0)])
    states = next_blocks(states, [cache_z1, cache_z3], [(1, 1), (3, 1)])
    states = next_blocks(states, [cache_z2], [(2, 1)], [weight_z[0], weight_a])
    joined_far = call(join_kernel, state_shape(own), [states[2], flip(states[3], "core")], 0)
    received, received_far = flip(states[1], "core"), flip(joined_far, "za")
    attention = call(
        finish_kernel,
        shape(queries.shape, bf16),
        [meta, test_lengths, states[0], received, received_far] + [weight_z[1]],
        2,
    )

    weight_z = [after(w, attention) for w in weight_z]
    weights = [out_weight, weight_a, *weight_z, *[flip(w, "za") for w in weight_z]]

    rows_y = [attention] + [from_y(attention, s) for s in (1, 2, 3)]
    rows_all = rows_y + [flip(r, "core") for r in rows_y]
    terms = lambda dtype: shape((2, 4 * rows, out_weight.shape[1]), dtype)
    keep_a, keep_b, send_a, send_b = call(
        project_kernel,
        [terms(f32), terms(f32), terms(bf16), terms(bf16)],
        [meta, *rows_all, *weights],
        1,
        2 * 8 * rows * out_weight.size * 4,
        scratch=[pltpu.VMEM((8 * rows, width), bf16), pltpu.VMEM((4,) + out_weight.shape, bf16)],
    )
    by_1 = lambda a: move(a, {"x": lambda c: c["x"] ^ 1})
    by_3 = lambda a: move(a, {"x": lambda c: c["x"] ^ 3})
    sum_a = keep_a + by_1(send_a).astype(f32)
    sum_b = keep_b + by_3(send_b).astype(f32)
    sum_a = sum_a[0] + by_3(sum_a[1])
    sum_b = sum_b[0] + by_1(sum_b[1])
    chunks = []
    for k, total in enumerate((sum_a, sum_b)):
        arrived = []
        for h in range(2):
            route = {
                "zb": lambda c: c["x"] % 2,
                "za": lambda c, k=k: c["za"] ^ k,
                "zh": lambda c, h=h: c["zh"] ^ h,
                "x": lambda c: c["x"] // 2 * 2 + c["zb"],
            }
            piece = total[h * 2 * rows : (h + 1) * 2 * rows]
            arrived.append(move(piece if h == k == 0 else piece.astype(bf16), route).astype(f32))
        chunks.append((arrived[0] + arrived[1]).astype(bf16))
    first = lax.axis_index("za") == 0
    return jnp.concatenate(
        [jnp.where(first, chunks[0], chunks[1]), jnp.where(first, chunks[1], chunks[0])], axis=0
    )


def solution(mesh):
    fine = Mesh(mesh.devices.reshape(tuple(SIZES.values())), tuple(SIZES))
    both = P(CTX, KVH)
    placed = (both, both, both, both, both, P(), P(), P(KVH, CTX))
    return jax.shard_map(
        per_device, mesh=fine, in_specs=placed, out_specs=P(KVH, CTX), check_vma=False
    )
```

```python
import functools
import itertools
import math

import jax
import jax.numpy as jnp
from jax import lax
from jax.experimental import pallas as pl
from jax.experimental.pallas import tpu as pltpu
from jax.sharding import Mesh
from jax.sharding import PartitionSpec as P

HEAD_DIM = 128
GROUP = 8
WINDOWS = 16
TLEN = 32
COLS = TLEN * GROUP
NEG_FILL = -1e30
SCALE = 1.0 / math.sqrt(HEAD_DIM)
LOG2E = math.log2(math.e)

SIZES = {"y": 4, "zb": 2, "za": 2, "core": 2, "zh": 2, "x": 4}
CTX = ("y", "zb", "za", "core")
KVH = ("zh", "x")
CTX_DEVICES = 32
TILE_FLOPS = 16
TOP, TOTAL, STATE_ROWS = HEAD_DIM, HEAD_DIM + 1, HEAD_DIM + 8
VMEM_LIMIT = 48 << 20
SMEM = pl.BlockSpec(memory_space=pltpu.SMEM)
VMEM = pl.BlockSpec(memory_space=pltpu.VMEM)
ANY = pl.BlockSpec(memory_space=pl.ANY)


def move(array, route):
    axes = tuple(route)
    places = list(itertools.product(*[range(SIZES[a]) for a in SIZES]))
    names = list(SIZES)
    pairs = set()
    index = lambda c: functools.reduce(lambda n, a: n * SIZES[a] + c[a], axes, 0)
    for place in places:
        c = dict(zip(names, place))
        pairs.add((index(c), index({a: route[a](c) for a in axes})))
    return lax.ppermute(array, axes, sorted(pairs))


def flip(array, *axes):
    return move(array, {a: (lambda c, a=a: c[a] ^ 1) for a in axes})


def from_y(array, shift):
    return move(array, {"y": lambda c: (c["y"] - shift) % SIZES["y"]})


def rounded(value):
    return value.astype(jnp.bfloat16).astype(jnp.float32)


def scores(keys, columns):
    return jnp.dot(keys, columns, preferred_element_type=jnp.float32)


def soften(dots, mask=None):
    if mask is not None:
        dots = jnp.where(mask, dots, NEG_FILL)
    top = rounded(jnp.max(dots, axis=0, keepdims=True) * SCALE)
    weights = jnp.exp2(dots * (SCALE * LOG2E) - top * LOG2E)
    if mask is not None:
        weights = jnp.where(mask, weights, 0.0)
    total = rounded(jnp.sum(weights, axis=0, keepdims=True))
    return top, total, weights.astype(jnp.bfloat16)


def block_out(values_t, total, weights):
    out = jnp.dot(values_t, weights, preferred_element_type=jnp.float32)
    return rounded(out * (1.0 / jnp.maximum(total, 0.5)))


def transposed(array):
    return array.astype(jnp.float32).T.astype(jnp.bfloat16)


def absorb(blocks, tiles, seen, columns, states):
    values = {}

    def finish(tile, top, total, weights):
        b, r, e = tile
        out = block_out(values[b], total, weights)
        visible = seen(b, r, e)
        top = jnp.where(visible, top, NEG_FILL)
        total = jnp.where(visible, total, 0.0)
        state_ref = states[r]
        old_top = state_ref[e, TOP : TOP + 1, :]
        joint = jnp.maximum(old_top, top)
        old = jnp.exp(old_top - joint)
        new = jnp.exp(top - joint) * total
        state_ref[e, :HEAD_DIM, :] = old * state_ref[e, :HEAD_DIM, :] + new * out
        state_ref[e, TOTAL : TOTAL + 1, :] = old * state_ref[e, TOTAL : TOTAL + 1, :] + new
        state_ref[e, TOP : TOP + 1, :] = joint

    def start(tile):
        b, r, e = tile
        if b not in values:
            values[b] = transposed(blocks[b][1])
        return scores(blocks[b][0], columns[r][e])

    ahead, behind = start(tiles[0]), None
    for n, tile in enumerate(tiles):
        dots = ahead
        if n + 1 < len(tiles):
            ahead = start(tiles[n + 1])
        softened = soften(dots)
        if behind is not None:
            finish(*behind)
        behind = (tile, *softened)
    finish(*behind)


def sees(meta_ref, select_ref, own_examples, sources):
    y, zb, za, core = [meta_ref[n] for n in range(4)]
    windows = []
    for far_y, far_zb in sources:
        block = (((y + far_y) % 4 * 2 + (zb ^ far_zb)) * 2 + za) * 2 + core
        windows.append(block * WINDOWS // CTX_DEVICES)
    place = ((y * 2 + zb) * 2 + za) * 2 + core

    def seen(b, r, e):
        return select_ref[(place ^ r) * own_examples + e, windows[b]] > 0

    return seen


def make_columns(q_ref, columns_ref):
    for e in range(q_ref.shape[0] // TLEN):
        rows = q_ref[e * TLEN : (e + 1) * TLEN, :]
        stacked = jnp.concatenate(
            [rows[:, h * HEAD_DIM : (h + 1) * HEAD_DIM] for h in range(GROUP)], axis=0
        )
        columns_ref[e] = transposed(stacked)


def own_kernel(meta_ref, select_ref, q_ref, test_ref, kv_ref, columns_ref, state_ref):
    own = q_ref.shape[0] // TLEN
    make_columns(q_ref, columns_ref)
    token = lax.broadcasted_iota(jnp.int32, (TLEN, COLS), 0)
    place = lax.broadcasted_iota(jnp.int32, (TLEN, COLS), 1) % TLEN
    for e in range(own):
        rows = pl.ds(e * TLEN, TLEN)
        dots = scores(test_ref[rows, :HEAD_DIM], columns_ref[e])
        top, total, weights = soften(dots, token <= place)
        out = block_out(transposed(test_ref[rows, HEAD_DIM:]), total, weights)
        state_ref[e, :HEAD_DIM, :] = total * out
        state_ref[e, TOP : TOP + 1, :] = top
        state_ref[e, TOTAL : TOTAL + 1, :] = total
    seen = sees(meta_ref, select_ref, own, [(0, 0)])
    tiles = [(0, 0, e) for e in range(own)]
    absorb([(kv_ref[0], kv_ref[1])], tiles, seen, [columns_ref], [state_ref])


def group_kernel(sources, meta_ref, select_ref, own_columns_ref, own_state_ref, *refs):
    queries, blocks, refs = refs[:3], refs[3 : 3 + len(sources)], refs[3 + len(sources) :]
    weight_ref, others, states, copy_ref, sem = refs[0], refs[1:4], refs[4:8], refs[8], refs[9]
    copy = pltpu.make_async_copy(weight_ref, copy_ref, sem)
    copy.start()
    own = own_state_ref.shape[0]
    states[0][...] = own_state_ref[...]
    empty = lax.broadcasted_iota(jnp.int32, (STATE_ROWS, COLS), 0) == TOP
    for r in range(3):
        make_columns(queries[r], others[r])
        for e in range(own):
            states[r + 1][e] = jnp.where(empty, NEG_FILL, 0.0)
    seen = sees(meta_ref, select_ref, own, sources)
    tiles = [(b, r, e) for b in range(len(blocks)) for r in range(b == 0, 4) for e in range(own)]
    pairs = [(ref[0], ref[1]) for ref in blocks]
    absorb(pairs, tiles, seen, [own_columns_ref, *others], states)
    copy.wait()


def next_kernel(sources, meta_ref, select_ref, *refs):
    columns, before, blocks, states = refs[:4], refs[4:8], refs[8 : 8 + len(sources)], refs[-4:]
    own = before[0].shape[0]
    for r in range(4):
        states[r][...] = before[r][...]
    seen = sees(meta_ref, select_ref, own, sources)
    tiles = [(b, r, e) for b in range(len(blocks)) for r in range(4) for e in range(own)]
    absorb([(ref[0], ref[1]) for ref in blocks], tiles, seen, columns, states)


def joined(parts):
    top = functools.reduce(jnp.maximum, [part[TOP : TOP + 1] for part in parts])
    total, over = 0.0, 0.0
    for part in parts:
        scale = jnp.exp(part[TOP : TOP + 1] - top)
        total = total + scale * part[TOTAL : TOTAL + 1]
        over = over + scale * part[:HEAD_DIM]
    return top, total, over


def join_kernel(far_ref, received_ref, out_ref):
    own = far_ref.shape[0]
    for e in range(own):
        top, total, over = joined([far_ref[e], received_ref[e]])
        out_ref[e, :HEAD_DIM, :] = over
        out_ref[e, TOP : TOP + 1, :] = top
        out_ref[e, TOTAL : TOTAL + 1, :] = total
        out_ref[e, TOTAL + 1 :, :] = jnp.zeros((STATE_ROWS - TOTAL - 1, COLS), jnp.float32)


def finish_kernel(meta_ref, length_ref, mine_ref, received_ref, far_ref, *tokens_and_out):
    out_ref = tokens_and_out[-1]
    own = mine_ref.shape[0]
    place = ((meta_ref[0] * 2 + meta_ref[1]) * 2 + meta_ref[2]) * 2 + meta_ref[3]
    slot = lax.broadcasted_iota(jnp.int32, (1, COLS), 1) % TLEN
    for e in range(own):
        top, total, over = joined([mine_ref[e], received_ref[e], far_ref[e]])
        live = slot < length_ref[place * own + e]
        result = jnp.where(live, over * (1.0 / total), 0.0).T
        for h in range(GROUP):
            out_ref[e * TLEN : (e + 1) * TLEN, h * HEAD_DIM : (h + 1) * HEAD_DIM] = result[
                h * TLEN : (h + 1) * TLEN, :
            ].astype(jnp.bfloat16)


def project_kernel(meta_ref, *refs):
    rows, weights, keep_refs, send_refs, lined_ref = refs[:8], refs[8:12], refs[12:14], refs[14:16], refs[16]
    y, zb, zh, x = [meta_ref[n] for n in (0, 1, 4, 5)]
    height, width = rows[0].shape[0], weights[0].shape[1]
    for n in range(8):
        row_y = (y + n % 4) % 4
        at = ((row_y // 2) ^ zh) * 4 + (x ^ (2 * (row_y % 2) + (zb ^ (n // 4))))
        lined_ref[pl.ds(pl.multiple_of(at * height, height), height), :] = rows[n][...]
    for n in range(4):
        terms = jnp.dot(lined_ref[...], weights[n][...], preferred_element_type=jnp.float32)
        lanes = slice(n * width, (n + 1) * width)
        for h in range(2):
            kept, sent = ((0, 3), (1, 2)) if h == 0 else ((0, 1), (3, 2))
            for d in range(4):
                part = terms[(h * 4 + d) * height : (h * 4 + d + 1) * height]
                if d in kept:
                    keep_refs[h][kept.index(d), :, lanes] = part
                else:
                    send_refs[h][sent.index(d), :, lanes] = part.astype(jnp.bfloat16)


def total_kernel(mine_ref, received_ref, *out_refs):
    width = out_refs[0].shape[1]
    for n in range(4):
        lanes = slice(n * width, (n + 1) * width)
        total = mine_ref[:, lanes] + received_ref[:, lanes].astype(jnp.float32)
        out_refs[n][...] = total.astype(jnp.bfloat16)


def assemble_kernel(meta_ref, *refs):
    out_ref = refs[4]
    height = refs[0].shape[0]
    for n in range(4):
        at = (meta_ref[2] * 2 + meta_ref[3]) ^ n
        out_ref[pl.ds(pl.multiple_of(at * height, height), height), :] = refs[n][...]


def call(kernel, out_shape, inputs, scalars, flops=0, scratch=(), anywhere=0):
    nbytes = sum(a.size * a.dtype.itemsize for a in inputs)
    many = isinstance(out_shape, (list, tuple))
    return pl.pallas_call(
        kernel,
        out_shape=out_shape,
        in_specs=[SMEM] * scalars + [VMEM] * (len(inputs) - scalars - anywhere) + [ANY] * anywhere,
        out_specs=[VMEM] * (len(out_shape) - anywhere) + [ANY] * anywhere if many else VMEM,
        scratch_shapes=list(scratch),
        compiler_params=pltpu.CompilerParams(vmem_limit_bytes=VMEM_LIMIT),
        cost_estimate=pl.CostEstimate(flops=flops, bytes_accessed=nbytes, transcendentals=0),
    )(*inputs)


def per_device(
    queries, cache_keys, cache_values, test_keys, test_values, window_select, test_lengths, out_weight
):
    bf16, f32 = jnp.bfloat16, jnp.float32
    shape = jax.ShapeDtypeStruct
    part = functools.partial
    rows, width = queries.shape
    own = rows // TLEN
    meta = jnp.stack([lax.axis_index(a) for a in SIZES]).astype(jnp.int32)
    scalars = [meta, window_select]
    tile_flops = TILE_FLOPS * COLS * cache_keys.shape[0] * HEAD_DIM
    columns_shape = lambda n: shape((n, HEAD_DIM, COLS), bf16)
    state_shape = lambda n: shape((n, STATE_ROWS, COLS), f32)

    cache = jnp.stack([cache_keys, cache_values])
    cache_z = flip(cache, "zb")
    cache_1, cache_3 = from_y(cache, 1), from_y(cache, 3)
    cache_2 = from_y(cache_1, 1)
    q_far = flip(queries, "za")
    q_near = flip(queries, "core")
    q_far_near = flip(q_far, "core")
    cache_z1, cache_z3 = from_y(cache_z, 1), from_y(cache_z, 3)
    cache_z2 = from_y(cache_z3, 3)

    own_columns, own_state = call(
        own_kernel,
        [columns_shape(own), state_shape(own)],
        scalars + [queries, jnp.concatenate([test_keys, test_values], axis=1), cache],
        2,
        2 * own * tile_flops,
    )
    outputs = call(
        part(group_kernel, [(0, 0), (1, 0), (3, 0)]),
        [columns_shape(own)] * 3 + [state_shape(own)] * 4 + [shape(out_weight.shape, bf16)],
        scalars + [own_columns, own_state, q_near, q_far, q_far_near, cache, cache_1, cache_3, out_weight],
        2,
        11 * own * tile_flops,
        scratch=[pltpu.SemaphoreType.DMA],
        anywhere=1,
    )
    columns, states, weight = [own_columns, *outputs[:3]], outputs[3:7], outputs[7]
    weight_a = flip(weight, "za")

    def next_blocks(states, blocks, sources, tokens=()):
        return call(
            part(next_kernel, sources),
            [state_shape(own)] * 4,
            scalars + [*columns, *states, *blocks, *tokens],
            2,
            4 * len(blocks) * own * tile_flops,
        )

    states = next_blocks(states, [cache_z, cache_2], [(0, 1), (2, 0)])
    states = next_blocks(states, [cache_z1, cache_z3], [(1, 1), (3, 1)])
    states = next_blocks(states, [cache_z2], [(2, 1)], [weight_a])
    joined_far = call(join_kernel, state_shape(own), [states[2], flip(states[3], "core")], 0)
    received, received_far = flip(states[1], "core"), flip(joined_far, "za")
    attention = call(
        finish_kernel,
        shape(queries.shape, bf16),
        [meta, test_lengths, states[0], received, received_far],
        2,
    )

    weights = [out_weight, flip(out_weight, "core"), weight_a, flip(weight_a, "core")]

    attention_z = flip(attention, "zb")
    rows_all = [a if s == 0 else from_y(a, s) for a in (attention, attention_z) for s in range(4)]
    terms = lambda dtype: shape((2, rows, 4 * out_weight.shape[1]), dtype)
    keep_a, keep_b, send_a, send_b = call(
        project_kernel,
        [terms(f32), terms(f32), terms(bf16), terms(bf16)],
        [meta, *rows_all, *weights],
        1,
        2 * 8 * rows * out_weight.size * 4,
        scratch=[pltpu.VMEM((8 * rows, width), bf16)],
    )
    by_1 = lambda a: move(a, {"x": lambda c: c["x"] ^ 1})
    by_3 = lambda a: move(a, {"x": lambda c: c["x"] ^ 3})
    sum_a = keep_a + by_1(send_a).astype(f32)
    sum_b = keep_b + by_3(send_b).astype(f32)
    sum_a = sum_a[0] + by_3(sum_a[1])
    sum_b = sum_b[0] + by_1(sum_b[1])
    block = shape((rows, out_weight.shape[1]), bf16)
    totals = call(total_kernel, [block] * 4, [sum_a, flip(sum_b.astype(bf16), "zh")], 0)
    arrived = [totals[0], flip(totals[1], "core"), flip(totals[2], "za"), flip(totals[3], "za", "core")]
    return call(assemble_kernel, shape((4 * rows, out_weight.shape[1]), bf16), [meta, *arrived], 1)


def solution(mesh):
    fine = Mesh(mesh.devices.reshape(tuple(SIZES.values())), tuple(SIZES))
    both = P(CTX, KVH)
    placed = (both, both, both, both, both, P(), P(), P(KVH, CTX))
    return jax.shard_map(
        per_device, mesh=fine, in_specs=placed, out_specs=P(KVH, CTX), check_vma=False
    )
```

```python
import functools
import itertools
import math

import jax
import jax.numpy as jnp
from jax import lax
from jax.experimental import pallas as pl
from jax.experimental.pallas import tpu as pltpu
from jax.sharding import Mesh
from jax.sharding import PartitionSpec as P

HEAD_DIM = 128
GROUP = 8
WINDOWS = 16
TLEN = 32
COLS = TLEN * GROUP
NEG_FILL = -1e30
SCALE = 1.0 / math.sqrt(HEAD_DIM)
LOG2E = math.log2(math.e)

SIZES = {"y": 4, "zb": 2, "za": 2, "core": 2, "zh": 2, "x": 4}
CTX = ("y", "zb", "za", "core")
KVH = ("zh", "x")
CTX_DEVICES = 32
TILE_FLOPS = 16
TOP, TOTAL, STATE_ROWS = HEAD_DIM, HEAD_DIM + 1, HEAD_DIM + 8
VMEM_LIMIT = 48 << 20
SMEM = pl.BlockSpec(memory_space=pltpu.SMEM)
VMEM = pl.BlockSpec(memory_space=pltpu.VMEM)
ANY = pl.BlockSpec(memory_space=pl.ANY)


def move(array, route):
    axes = tuple(route)
    places = list(itertools.product(*[range(SIZES[a]) for a in SIZES]))
    names = list(SIZES)
    pairs = set()
    index = lambda c: functools.reduce(lambda n, a: n * SIZES[a] + c[a], axes, 0)
    for place in places:
        c = dict(zip(names, place))
        pairs.add((index(c), index({a: route[a](c) for a in axes})))
    return lax.ppermute(array, axes, sorted(pairs))


def flip(array, *axes):
    return move(array, {a: (lambda c, a=a: c[a] ^ 1) for a in axes})


def from_y(array, shift):
    return move(array, {"y": lambda c: (c["y"] - shift) % SIZES["y"]})


def after(array, token):
    def kernel(array_ref, token_ref, out_ref):
        pass

    return pl.pallas_call(
        kernel,
        out_shape=jax.ShapeDtypeStruct(array.shape, array.dtype),
        in_specs=[ANY, ANY],
        out_specs=ANY,
        input_output_aliases={0: 0},
    )(array, token)


def rounded(value):
    return value.astype(jnp.bfloat16).astype(jnp.float32)


def scores(keys, columns):
    return jnp.dot(keys, columns, preferred_element_type=jnp.float32)


def soften(dots, mask=None):
    if mask is not None:
        dots = jnp.where(mask, dots, NEG_FILL)
    top = rounded(jnp.max(dots, axis=0, keepdims=True) * SCALE)
    weights = jnp.exp2(dots * (SCALE * LOG2E) - top * LOG2E)
    if mask is not None:
        weights = jnp.where(mask, weights, 0.0)
    total = rounded(jnp.sum(weights, axis=0, keepdims=True))
    return top, total, weights.astype(jnp.bfloat16)


def block_out(values_t, total, weights):
    out = jnp.dot(values_t, weights, preferred_element_type=jnp.float32)
    return rounded(out * (1.0 / jnp.maximum(total, 0.5)))


def transposed(array):
    return array.astype(jnp.float32).T.astype(jnp.bfloat16)


def absorb(blocks, tiles, seen, columns, states):
    values = {}

    def finish(tile, top, total, weights):
        b, r, e = tile
        out = block_out(values[b], total, weights)
        visible = seen(b, r, e)
        top = jnp.where(visible, top, NEG_FILL)
        total = jnp.where(visible, total, 0.0)
        state_ref = states[r]
        old_top = state_ref[e, TOP : TOP + 1, :]
        joint = jnp.maximum(old_top, top)
        old = jnp.exp(old_top - joint)
        new = jnp.exp(top - joint) * total
        state_ref[e, :HEAD_DIM, :] = old * state_ref[e, :HEAD_DIM, :] + new * out
        state_ref[e, TOTAL : TOTAL + 1, :] = old * state_ref[e, TOTAL : TOTAL + 1, :] + new
        state_ref[e, TOP : TOP + 1, :] = joint

    def start(tile):
        b, r, e = tile
        if b not in values:
            values[b] = transposed(blocks[b][1])
        return scores(blocks[b][0], columns[r][e])

    ahead, behind = start(tiles[0]), None
    for n, tile in enumerate(tiles):
        dots = ahead
        if n + 1 < len(tiles):
            ahead = start(tiles[n + 1])
        softened = soften(dots)
        if behind is not None:
            finish(*behind)
        behind = (tile, *softened)
    finish(*behind)


def sees(meta_ref, select_ref, own_examples, sources):
    y, zb, za, core = [meta_ref[n] for n in range(4)]
    windows = []
    for far_y, far_zb in sources:
        block = (((y + far_y) % 4 * 2 + (zb ^ far_zb)) * 2 + za) * 2 + core
        windows.append(block * WINDOWS // CTX_DEVICES)
    place = ((y * 2 + zb) * 2 + za) * 2 + core

    def seen(b, r, e):
        return select_ref[(place ^ r) * own_examples + e, windows[b]] > 0

    return seen


def make_columns(q_ref, columns_ref):
    for e in range(q_ref.shape[0] // TLEN):
        rows = q_ref[e * TLEN : (e + 1) * TLEN, :]
        stacked = jnp.concatenate(
            [rows[:, h * HEAD_DIM : (h + 1) * HEAD_DIM] for h in range(GROUP)], axis=0
        )
        columns_ref[e] = transposed(stacked)


def own_kernel(meta_ref, select_ref, q_ref, test_ref, kv_ref, columns_ref, state_ref):
    own = q_ref.shape[0] // TLEN
    make_columns(q_ref, columns_ref)
    token = lax.broadcasted_iota(jnp.int32, (TLEN, COLS), 0)
    place = lax.broadcasted_iota(jnp.int32, (TLEN, COLS), 1) % TLEN
    for e in range(own):
        rows = pl.ds(e * TLEN, TLEN)
        dots = scores(test_ref[rows, :HEAD_DIM], columns_ref[e])
        top, total, weights = soften(dots, token <= place)
        out = block_out(transposed(test_ref[rows, HEAD_DIM:]), total, weights)
        state_ref[e, :HEAD_DIM, :] = total * out
        state_ref[e, TOP : TOP + 1, :] = top
        state_ref[e, TOTAL : TOTAL + 1, :] = total
    seen = sees(meta_ref, select_ref, own, [(0, 0)])
    tiles = [(0, 0, e) for e in range(own)]
    absorb([(kv_ref[0], kv_ref[1])], tiles, seen, [columns_ref], [state_ref])


def group_kernel(sources, meta_ref, select_ref, own_columns_ref, own_state_ref, *refs):
    queries, blocks, refs = refs[:3], refs[3 : 3 + len(sources)], refs[3 + len(sources) :]
    weight_ref, others, states, copy_ref, sem = refs[0], refs[1:4], refs[4:8], refs[8], refs[9]
    copy = pltpu.make_async_copy(weight_ref, copy_ref, sem)
    copy.start()
    own = own_state_ref.shape[0]
    states[0][...] = own_state_ref[...]
    empty = lax.broadcasted_iota(jnp.int32, (STATE_ROWS, COLS), 0) == TOP
    for r in range(3):
        make_columns(queries[r], others[r])
        for e in range(own):
            states[r + 1][e] = jnp.where(empty, NEG_FILL, 0.0)
    seen = sees(meta_ref, select_ref, own, sources)
    tiles = [(b, r, e) for b in range(len(blocks)) for r in range(b == 0, 4) for e in range(own)]
    pairs = [(ref[0], ref[1]) for ref in blocks]
    absorb(pairs, tiles, seen, [own_columns_ref, *others], states)
    copy.wait()


def next_kernel(sources, members, skipped, meta_ref, select_ref, *refs):
    count = len(members)
    columns, before = refs[:count], refs[count : 2 * count]
    blocks, states = refs[2 * count : 2 * count + len(sources)], refs[-count:]
    own = before[0].shape[0]
    for n in range(count):
        states[n][...] = before[n][...]
    seen = sees(meta_ref, select_ref, own, sources)
    tiles = [
        (b, n, e)
        for b in range(len(blocks))
        for n in range(count)
        for e in range(own)
        if (b, members[n]) not in skipped
    ]
    pairs = [(ref[0], ref[1]) for ref in blocks]
    absorb(pairs, tiles, lambda b, n, e: seen(b, members[n], e), columns, states)


def joined(parts):
    top = functools.reduce(jnp.maximum, [part[TOP : TOP + 1] for part in parts])
    total, over = 0.0, 0.0
    for part in parts:
        scale = jnp.exp(part[TOP : TOP + 1] - top)
        total = total + scale * part[TOTAL : TOTAL + 1]
        over = over + scale * part[:HEAD_DIM]
    return top, total, over


def join_kernel(far_ref, received_ref, out_ref):
    own = far_ref.shape[0]
    for e in range(own):
        top, total, over = joined([far_ref[e], received_ref[e]])
        out_ref[e, :HEAD_DIM, :] = over
        out_ref[e, TOP : TOP + 1, :] = top
        out_ref[e, TOTAL : TOTAL + 1, :] = total
        out_ref[e, TOTAL + 1 :, :] = jnp.zeros((STATE_ROWS - TOTAL - 1, COLS), jnp.float32)


def finish_kernel(meta_ref, length_ref, mine_ref, received_ref, far_ref, *tokens_and_out):
    out_ref = tokens_and_out[-1]
    own = mine_ref.shape[0]
    place = ((meta_ref[0] * 2 + meta_ref[1]) * 2 + meta_ref[2]) * 2 + meta_ref[3]
    slot = lax.broadcasted_iota(jnp.int32, (1, COLS), 1) % TLEN
    for e in range(own):
        top, total, over = joined([mine_ref[e], received_ref[e], far_ref[e]])
        live = slot < length_ref[place * own + e]
        result = jnp.where(live, over * (1.0 / total), 0.0).T
        for h in range(GROUP):
            out_ref[e * TLEN : (e + 1) * TLEN, h * HEAD_DIM : (h + 1) * HEAD_DIM] = result[
                h * TLEN : (h + 1) * TLEN, :
            ].astype(jnp.bfloat16)


def project_kernel(meta_ref, *refs):
    rows, weights, keep_refs, send_refs, lined_ref = refs[:8], refs[8:12], refs[12:14], refs[14:16], refs[16]
    y, zb, zh, x = [meta_ref[n] for n in (0, 1, 4, 5)]
    height, width = rows[0].shape[0], weights[0].shape[1]
    for n in range(8):
        row_y = (y + n % 4) % 4
        at = ((row_y // 2) ^ zh) * 4 + (x ^ (2 * (row_y % 2) + (zb ^ (n // 4))))
        lined_ref[pl.ds(pl.multiple_of(at * height, height), height), :] = rows[n][...]
    for n in range(4):
        terms = jnp.dot(lined_ref[...], weights[n][...], preferred_element_type=jnp.float32)
        lanes = slice(n * width, (n + 1) * width)
        for h in range(2):
            kept, sent = ((0, 3), (1, 2)) if h == 0 else ((0, 1), (3, 2))
            for d in range(4):
                part = terms[(h * 4 + d) * height : (h * 4 + d + 1) * height]
                if d in kept:
                    keep_refs[h][kept.index(d), :, lanes] = part
                else:
                    send_refs[h][sent.index(d), :, lanes] = part.astype(jnp.bfloat16)


def total_kernel(mine_ref, received_ref, *out_refs):
    width = out_refs[0].shape[1]
    for n in range(4):
        lanes = slice(n * width, (n + 1) * width)
        total = mine_ref[:, lanes] + received_ref[:, lanes].astype(jnp.float32)
        out_refs[n][...] = total.astype(jnp.bfloat16)


def assemble_kernel(meta_ref, *refs):
    out_ref = refs[4]
    height = refs[0].shape[0]
    for n in range(4):
        at = (meta_ref[2] * 2 + meta_ref[3]) ^ n
        out_ref[pl.ds(pl.multiple_of(at * height, height), height), :] = refs[n][...]


def call(kernel, out_shape, inputs, scalars, flops=0, scratch=(), anywhere=0):
    nbytes = sum(a.size * a.dtype.itemsize for a in inputs)
    many = isinstance(out_shape, (list, tuple))
    return pl.pallas_call(
        kernel,
        out_shape=out_shape,
        in_specs=[SMEM] * scalars + [VMEM] * (len(inputs) - scalars - anywhere) + [ANY] * anywhere,
        out_specs=[VMEM] * (len(out_shape) - anywhere) + [ANY] * anywhere if many else VMEM,
        scratch_shapes=list(scratch),
        compiler_params=pltpu.CompilerParams(vmem_limit_bytes=VMEM_LIMIT),
        cost_estimate=pl.CostEstimate(flops=flops, bytes_accessed=nbytes, transcendentals=0),
    )(*inputs)


def per_device(
    queries, cache_keys, cache_values, test_keys, test_values, window_select, test_lengths, out_weight
):
    bf16, f32 = jnp.bfloat16, jnp.float32
    shape = jax.ShapeDtypeStruct
    part = functools.partial
    rows, width = queries.shape
    own = rows // TLEN
    meta = jnp.stack([lax.axis_index(a) for a in SIZES]).astype(jnp.int32)
    scalars = [meta, window_select]
    tile_flops = TILE_FLOPS * COLS * cache_keys.shape[0] * HEAD_DIM
    columns_shape = lambda n: shape((n, HEAD_DIM, COLS), bf16)
    state_shape = lambda n: shape((n, STATE_ROWS, COLS), f32)

    cache = jnp.stack([cache_keys, cache_values])
    cache_z = flip(cache, "zb")
    cache_1, cache_3 = from_y(cache, 1), from_y(cache, 3)
    cache_2 = from_y(cache_1, 1)
    q_far = flip(queries, "za")
    q_near = flip(queries, "core")
    q_far_near = flip(q_far, "core")

    own_columns, own_state = call(
        own_kernel,
        [columns_shape(own), state_shape(own)],
        scalars + [queries, jnp.concatenate([test_keys, test_values], axis=1), cache],
        2,
        2 * own * tile_flops,
    )
    outputs = call(
        part(group_kernel, [(0, 0), (1, 0), (3, 0)]),
        [columns_shape(own)] * 3 + [state_shape(own)] * 4 + [shape(out_weight.shape, bf16)],
        scalars + [own_columns, own_state, q_near, q_far, q_far_near, cache, cache_1, cache_3, out_weight],
        2,
        11 * own * tile_flops,
        scratch=[pltpu.SemaphoreType.DMA],
        anywhere=1,
    )
    columns, states, weight = [own_columns, *outputs[:3]], outputs[3:7], outputs[7]
    cache_z = after(cache_z, states[0])
    cache_z1, cache_z3, cache_z2 = [from_y(cache_z, n) for n in (1, 3, 2)]
    weight_a = flip(weight, "za")

    def next_blocks(states, members, blocks, sources, skipped=(), tokens=()):
        before = [states[r] for r in members]
        after_them = call(
            part(next_kernel, sources, members, skipped),
            [state_shape(own)] * len(members),
            scalars + [columns[r] for r in members] + before + blocks + list(tokens),
            2,
            len(members) * len(blocks) * own * tile_flops,
        )
        for n, r in enumerate(members):
            states[r] = after_them[n]

    blocks, places = [cache_z1, cache_z3, cache_z2], [(1, 1), (3, 1), (2, 1)]
    states = list(states)
    next_blocks(states, (0, 1, 2, 3), [cache_z, cache_2], [(0, 1), (2, 0)])
    next_blocks(states, (2, 3), blocks, places, (), [weight_a])
    joined_far = call(join_kernel, state_shape(own), [states[2], flip(states[3], "core")], 0)
    received_far = flip(joined_far, "za")
    next_blocks(states, (0, 1), blocks, places, ((2, 0),), [joined_far])
    received = flip(states[1], "core")
    next_blocks(states, (0,), blocks[2:], places[2:], (), [received_far])
    attention = call(
        finish_kernel,
        shape(queries.shape, bf16),
        [meta, test_lengths, states[0], received, received_far],
        2,
    )

    weights = [out_weight, flip(out_weight, "core"), weight_a, flip(weight_a, "core")]

    attention_z = flip(attention, "zb")
    rows_all = [a if s == 0 else from_y(a, s) for a in (attention, attention_z) for s in range(4)]
    terms = lambda dtype: shape((2, rows, 4 * out_weight.shape[1]), dtype)
    keep_a, keep_b, send_a, send_b = call(
        project_kernel,
        [terms(f32), terms(f32), terms(bf16), terms(bf16)],
        [meta, *rows_all, *weights],
        1,
        2 * 8 * rows * out_weight.size * 4,
        scratch=[pltpu.VMEM((8 * rows, width), bf16)],
    )
    by_1 = lambda a: move(a, {"x": lambda c: c["x"] ^ 1})
    by_3 = lambda a: move(a, {"x": lambda c: c["x"] ^ 3})
    sum_a = keep_a + by_1(send_a).astype(f32)
    sum_b = keep_b + by_3(send_b).astype(f32)
    sum_a = sum_a[0] + by_3(sum_a[1])
    sum_b = sum_b[0] + by_1(sum_b[1])
    block = shape((rows, out_weight.shape[1]), bf16)
    totals = call(total_kernel, [block] * 4, [sum_a, flip(sum_b.astype(bf16), "zh")], 0)
    arrived = [totals[0], flip(totals[1], "core"), flip(totals[2], "za"), flip(totals[3], "za", "core")]
    return call(assemble_kernel, shape((4 * rows, out_weight.shape[1]), bf16), [meta, *arrived], 1)


def solution(mesh):
    fine = Mesh(mesh.devices.reshape(tuple(SIZES.values())), tuple(SIZES))
    both = P(CTX, KVH)
    placed = (both, both, both, both, both, P(), P(), P(KVH, CTX))
    return jax.shard_map(
        per_device, mesh=fine, in_specs=placed, out_specs=P(KVH, CTX), check_vma=False
    )
```

```python
import functools
import itertools
import math

import jax
import jax.numpy as jnp
from jax import lax
from jax.experimental import pallas as pl
from jax.experimental.pallas import tpu as pltpu
from jax.sharding import Mesh
from jax.sharding import PartitionSpec as P

HEAD_DIM = 128
GROUP = 8
WINDOWS = 16
TLEN = 32
COLS = TLEN * GROUP
NEG_FILL = -1e30
SCALE = 1.0 / math.sqrt(HEAD_DIM)
LOG2E = math.log2(math.e)

SIZES = {"y": 4, "zb": 2, "za": 2, "core": 2, "zh": 2, "x": 4}
CTX = ("y", "zb", "za", "core")
KVH = ("zh", "x")
CTX_DEVICES = 32
TILE_FLOPS = 16
TOP, TOTAL, STATE_ROWS = HEAD_DIM, HEAD_DIM + 1, HEAD_DIM + 8
VMEM_LIMIT = 48 << 20
SMEM = pl.BlockSpec(memory_space=pltpu.SMEM)
VMEM = pl.BlockSpec(memory_space=pltpu.VMEM)
ANY = pl.BlockSpec(memory_space=pl.ANY)


def move(array, route):
    axes = tuple(route)
    places = list(itertools.product(*[range(SIZES[a]) for a in SIZES]))
    names = list(SIZES)
    pairs = set()
    index = lambda c: functools.reduce(lambda n, a: n * SIZES[a] + c[a], axes, 0)
    for place in places:
        c = dict(zip(names, place))
        pairs.add((index(c), index({a: route[a](c) for a in axes})))
    return lax.ppermute(array, axes, sorted(pairs))


def flip(array, *axes):
    return move(array, {a: (lambda c, a=a: c[a] ^ 1) for a in axes})


def from_y(array, shift):
    return move(array, {"y": lambda c: (c["y"] - shift) % SIZES["y"]})


def after(array, token):
    def kernel(array_ref, token_ref, out_ref):
        pass

    return pl.pallas_call(
        kernel,
        out_shape=jax.ShapeDtypeStruct(array.shape, array.dtype),
        in_specs=[ANY, ANY],
        out_specs=ANY,
        input_output_aliases={0: 0},
        compiler_params=pltpu.CompilerParams(vmem_limit_bytes=1 << 20),
    )(array, token)


def rounded(value):
    return value.astype(jnp.bfloat16).astype(jnp.float32)


def scores(keys, columns):
    return jnp.dot(keys, columns, preferred_element_type=jnp.float32)


def soften(dots, mask=None):
    if mask is not None:
        dots = jnp.where(mask, dots, NEG_FILL)
    top = rounded(jnp.max(dots, axis=0, keepdims=True) * SCALE)
    weights = jnp.exp2(dots * (SCALE * LOG2E) - top * LOG2E)
    if mask is not None:
        weights = jnp.where(mask, weights, 0.0)
    total = rounded(jnp.sum(weights, axis=0, keepdims=True))
    return top, total, weights.astype(jnp.bfloat16)


def block_out(values_t, total, weights):
    out = jnp.dot(values_t, weights, preferred_element_type=jnp.float32)
    return rounded(out * (1.0 / jnp.maximum(total, 0.5)))


def transposed(array):
    return array.astype(jnp.float32).T.astype(jnp.bfloat16)


def absorb(blocks, tiles, seen, columns, states):
    values = {}

    def finish(tile, top, total, weights):
        b, r, e = tile
        out = block_out(values[b], total, weights)
        visible = seen(b, r, e)
        top = jnp.where(visible, top, NEG_FILL)
        total = jnp.where(visible, total, 0.0)
        state_ref = states[r]
        old_top = state_ref[e, TOP : TOP + 1, :]
        joint = jnp.maximum(old_top, top)
        old = jnp.exp(old_top - joint)
        new = jnp.exp(top - joint) * total
        state_ref[e, :HEAD_DIM, :] = old * state_ref[e, :HEAD_DIM, :] + new * out
        state_ref[e, TOTAL : TOTAL + 1, :] = old * state_ref[e, TOTAL : TOTAL + 1, :] + new
        state_ref[e, TOP : TOP + 1, :] = joint

    def start(tile):
        b, r, e = tile
        if b not in values:
            values[b] = transposed(blocks[b][1])
        return scores(blocks[b][0], columns[r][e])

    ahead, behind = start(tiles[0]), None
    for n, tile in enumerate(tiles):
        dots = ahead
        if n + 1 < len(tiles):
            ahead = start(tiles[n + 1])
        softened = soften(dots)
        if behind is not None:
            finish(*behind)
        behind = (tile, *softened)
    finish(*behind)


def sees(meta_ref, select_ref, own_examples, sources):
    y, zb, za, core = [meta_ref[n] for n in range(4)]
    windows = []
    for far_y, far_zb in sources:
        block = (((y + far_y) % 4 * 2 + (zb ^ far_zb)) * 2 + za) * 2 + core
        windows.append(block * WINDOWS // CTX_DEVICES)
    place = ((y * 2 + zb) * 2 + za) * 2 + core

    def seen(b, r, e):
        return select_ref[(place ^ r) * own_examples + e, windows[b]] > 0

    return seen


def make_columns(q_ref, columns_ref):
    for e in range(q_ref.shape[0] // TLEN):
        rows = q_ref[e * TLEN : (e + 1) * TLEN, :]
        stacked = jnp.concatenate(
            [rows[:, h * HEAD_DIM : (h + 1) * HEAD_DIM] for h in range(GROUP)], axis=0
        )
        columns_ref[e] = transposed(stacked)


def own_kernel(meta_ref, select_ref, q_ref, test_ref, kv_ref, columns_ref, state_ref):
    own = q_ref.shape[0] // TLEN
    make_columns(q_ref, columns_ref)
    token = lax.broadcasted_iota(jnp.int32, (TLEN, COLS), 0)
    place = lax.broadcasted_iota(jnp.int32, (TLEN, COLS), 1) % TLEN
    for e in range(own):
        rows = pl.ds(e * TLEN, TLEN)
        dots = scores(test_ref[rows, :HEAD_DIM], columns_ref[e])
        top, total, weights = soften(dots, token <= place)
        out = block_out(transposed(test_ref[rows, HEAD_DIM:]), total, weights)
        state_ref[e, :HEAD_DIM, :] = total * out
        state_ref[e, TOP : TOP + 1, :] = top
        state_ref[e, TOTAL : TOTAL + 1, :] = total
    seen = sees(meta_ref, select_ref, own, [(0, 0)])
    tiles = [(0, 0, e) for e in range(own)]
    absorb([(kv_ref[0], kv_ref[1])], tiles, seen, [columns_ref], [state_ref])


def group_kernel(sources, meta_ref, select_ref, own_columns_ref, own_state_ref, *refs):
    queries, blocks, refs = refs[:3], refs[3 : 3 + len(sources)], refs[3 + len(sources) :]
    weight_ref, others, states, copy_ref, sem = refs[0], refs[1:4], refs[4:8], refs[8], refs[9]
    copy = pltpu.make_async_copy(weight_ref, copy_ref, sem)
    copy.start()
    own = own_state_ref.shape[0]
    states[0][...] = own_state_ref[...]
    empty = lax.broadcasted_iota(jnp.int32, (STATE_ROWS, COLS), 0) == TOP
    for r in range(3):
        make_columns(queries[r], others[r])
        for e in range(own):
            states[r + 1][e] = jnp.where(empty, NEG_FILL, 0.0)
    seen = sees(meta_ref, select_ref, own, sources)
    tiles = [(b, r, e) for b in range(len(blocks)) for r in range(b == 0, 4) for e in range(own)]
    pairs = [(ref[0], ref[1]) for ref in blocks]
    absorb(pairs, tiles, seen, [own_columns_ref, *others], states)
    copy.wait()


def next_kernel(sources, members, skipped, meta_ref, select_ref, *refs):
    count = len(members)
    columns, before = refs[:count], refs[count : 2 * count]
    blocks, states = refs[2 * count : 2 * count + len(sources)], refs[-count:]
    own = before[0].shape[0]
    for n in range(count):
        states[n][...] = before[n][...]
    seen = sees(meta_ref, select_ref, own, sources)
    tiles = [
        (b, n, e)
        for b in range(len(blocks))
        for n in range(count)
        for e in range(own)
        if (b, members[n]) not in skipped
    ]
    pairs = [(ref[0], ref[1]) for ref in blocks]
    absorb(pairs, tiles, lambda b, n, e: seen(b, members[n], e), columns, states)


def joined(parts):
    top = functools.reduce(jnp.maximum, [part[TOP : TOP + 1] for part in parts])
    total, over = 0.0, 0.0
    for part in parts:
        scale = jnp.exp(part[TOP : TOP + 1] - top)
        total = total + scale * part[TOTAL : TOTAL + 1]
        over = over + scale * part[:HEAD_DIM]
    return top, total, over


def join_kernel(far_ref, received_ref, out_ref):
    own = far_ref.shape[0]
    for e in range(own):
        top, total, over = joined([far_ref[e], received_ref[e]])
        out_ref[e, :HEAD_DIM, :] = over
        out_ref[e, TOP : TOP + 1, :] = top
        out_ref[e, TOTAL : TOTAL + 1, :] = total
        out_ref[e, TOTAL + 1 :, :] = jnp.zeros((STATE_ROWS - TOTAL - 1, COLS), jnp.float32)


def finish_kernel(meta_ref, length_ref, mine_ref, received_ref, far_ref, *tokens_and_out):
    out_ref = tokens_and_out[-1]
    own = mine_ref.shape[0]
    place = ((meta_ref[0] * 2 + meta_ref[1]) * 2 + meta_ref[2]) * 2 + meta_ref[3]
    slot = lax.broadcasted_iota(jnp.int32, (1, COLS), 1) % TLEN
    for e in range(own):
        top, total, over = joined([mine_ref[e], received_ref[e], far_ref[e]])
        live = slot < length_ref[place * own + e]
        result = jnp.where(live, over * (1.0 / total), 0.0).T
        for h in range(GROUP):
            out_ref[e * TLEN : (e + 1) * TLEN, h * HEAD_DIM : (h + 1) * HEAD_DIM] = result[
                h * TLEN : (h + 1) * TLEN, :
            ].astype(jnp.bfloat16)


def project_kernel(meta_ref, *refs):
    rows, weights, keep_refs, send_refs, lined_ref = refs[:8], refs[8:12], refs[12:14], refs[14:16], refs[16]
    y, zb, zh, x = [meta_ref[n] for n in (0, 1, 4, 5)]
    height, width = rows[0].shape[0], weights[0].shape[1]
    for n in range(8):
        row_y = (y + n % 4) % 4
        at = ((row_y // 2) ^ zh) * 4 + (x ^ (2 * (row_y % 2) + (zb ^ (n // 4))))
        lined_ref[pl.ds(pl.multiple_of(at * height, height), height), :] = rows[n][...]
    for n in range(4):
        terms = jnp.dot(lined_ref[...], weights[n][...], preferred_element_type=jnp.float32)
        lanes = slice(n * width, (n + 1) * width)
        for h in range(2):
            kept, sent = ((0, 3), (1, 2)) if h == 0 else ((0, 1), (3, 2))
            for d in range(4):
                part = terms[(h * 4 + d) * height : (h * 4 + d + 1) * height]
                if d in kept:
                    keep_refs[h][kept.index(d), :, lanes] = part
                else:
                    send_refs[h][sent.index(d), :, lanes] = part.astype(jnp.bfloat16)


def total_kernel(mine_ref, received_ref, *out_refs):
    width = out_refs[0].shape[1]
    for n in range(4):
        lanes = slice(n * width, (n + 1) * width)
        total = mine_ref[:, lanes] + received_ref[:, lanes].astype(jnp.float32)
        out_refs[n][...] = total.astype(jnp.bfloat16)


def assemble_kernel(meta_ref, *refs):
    out_ref = refs[4]
    height = refs[0].shape[0]
    for n in range(4):
        at = (meta_ref[2] * 2 + meta_ref[3]) ^ n
        out_ref[pl.ds(pl.multiple_of(at * height, height), height), :] = refs[n][...]


def call(kernel, out_shape, inputs, scalars, flops=0, scratch=(), anywhere=0):
    nbytes = sum(a.size * a.dtype.itemsize for a in inputs)
    many = isinstance(out_shape, (list, tuple))
    return pl.pallas_call(
        kernel,
        out_shape=out_shape,
        in_specs=[SMEM] * scalars + [VMEM] * (len(inputs) - scalars - anywhere) + [ANY] * anywhere,
        out_specs=[VMEM] * (len(out_shape) - anywhere) + [ANY] * anywhere if many else VMEM,
        scratch_shapes=list(scratch),
        compiler_params=pltpu.CompilerParams(vmem_limit_bytes=VMEM_LIMIT),
        cost_estimate=pl.CostEstimate(flops=flops, bytes_accessed=nbytes, transcendentals=0),
    )(*inputs)


def per_device(
    queries, cache_keys, cache_values, test_keys, test_values, window_select, test_lengths, out_weight
):
    bf16, f32 = jnp.bfloat16, jnp.float32
    shape = jax.ShapeDtypeStruct
    part = functools.partial
    rows, width = queries.shape
    own = rows // TLEN
    meta = jnp.stack([lax.axis_index(a) for a in SIZES]).astype(jnp.int32)
    scalars = [meta, window_select]
    tile_flops = TILE_FLOPS * COLS * cache_keys.shape[0] * HEAD_DIM
    columns_shape = lambda n: shape((n, HEAD_DIM, COLS), bf16)
    state_shape = lambda n: shape((n, STATE_ROWS, COLS), f32)

    cache = jnp.stack([cache_keys, cache_values])
    cache_z = flip(cache, "zb")
    cache_1, cache_3 = from_y(cache, 1), from_y(cache, 3)
    cache_2 = from_y(cache_1, 1)
    q_far = flip(queries, "za")
    q_near = flip(queries, "core")
    q_far_near = flip(q_far, "core")

    own_columns, own_state = call(
        own_kernel,
        [columns_shape(own), state_shape(own)],
        scalars + [queries, jnp.concatenate([test_keys, test_values], axis=1), cache],
        2,
        2 * own * tile_flops,
    )
    outputs = call(
        part(group_kernel, [(0, 0), (1, 0), (3, 0)]),
        [columns_shape(own)] * 3 + [state_shape(own)] * 4 + [shape(out_weight.shape, bf16)],
        scalars + [own_columns, own_state, q_near, q_far, q_far_near, cache, cache_1, cache_3, out_weight],
        2,
        11 * own * tile_flops,
        scratch=[pltpu.SemaphoreType.DMA],
        anywhere=1,
    )
    columns, states, weight = [own_columns, *outputs[:3]], outputs[3:7], outputs[7]
    cache_z = after(cache_z, states[0])
    cache_z1, cache_z3, cache_z2 = [from_y(cache_z, n) for n in (1, 3, 2)]
    weight_a = flip(weight, "za")

    def next_blocks(states, members, blocks, sources, skipped=(), tokens=()):
        before = [states[r] for r in members]
        after_them = call(
            part(next_kernel, sources, members, skipped),
            [state_shape(own)] * len(members),
            scalars + [columns[r] for r in members] + before + blocks + list(tokens),
            2,
            len(members) * len(blocks) * own * tile_flops,
        )
        for n, r in enumerate(members):
            states[r] = after_them[n]

    blocks, places = [cache_z1, cache_z3, cache_z2], [(1, 1), (3, 1), (2, 1)]
    states = list(states)
    next_blocks(states, (0, 1, 2, 3), [cache_z, cache_2], [(0, 1), (2, 0)])
    next_blocks(states, (2, 3), blocks, places, (), [weight_a])
    joined_far = call(join_kernel, state_shape(own), [states[2], flip(states[3], "core")], 0)
    received_far = flip(joined_far, "za")
    next_blocks(states, (0, 1), blocks, places, ((2, 0),), [joined_far])
    received = flip(states[1], "core")
    next_blocks(states, (0,), blocks[2:], places[2:], (), [received_far])
    attention = call(
        finish_kernel,
        shape(queries.shape, bf16),
        [meta, test_lengths, states[0], received, received_far],
        2,
    )

    weights = [out_weight, flip(out_weight, "core"), weight_a, flip(weight_a, "core")]

    attention_z = flip(attention, "zb")
    rows_all = [a if s == 0 else from_y(a, s) for a in (attention, attention_z) for s in range(4)]
    terms = lambda dtype: shape((2, rows, 4 * out_weight.shape[1]), dtype)
    keep_a, keep_b, send_a, send_b = call(
        project_kernel,
        [terms(f32), terms(f32), terms(bf16), terms(bf16)],
        [meta, *rows_all, *weights],
        1,
        2 * 8 * rows * out_weight.size * 4,
        scratch=[pltpu.VMEM((8 * rows, width), bf16)],
    )
    by_1 = lambda a: move(a, {"x": lambda c: c["x"] ^ 1})
    by_3 = lambda a: move(a, {"x": lambda c: c["x"] ^ 3})
    sum_a = keep_a + by_1(send_a).astype(f32)
    sum_b = keep_b + by_3(send_b).astype(f32)
    sum_a = sum_a[0] + by_3(sum_a[1])
    sum_b = sum_b[0] + by_1(sum_b[1])
    block = shape((rows, out_weight.shape[1]), bf16)
    totals = call(total_kernel, [block] * 4, [sum_a, flip(sum_b.astype(bf16), "zh")], 0)
    arrived = [totals[0], flip(totals[1], "core"), flip(totals[2], "za"), flip(totals[3], "za", "core")]
    return call(assemble_kernel, shape((4 * rows, out_weight.shape[1]), bf16), [meta, *arrived], 1)


def solution(mesh):
    fine = Mesh(mesh.devices.reshape(tuple(SIZES.values())), tuple(SIZES))
    both = P(CTX, KVH)
    placed = (both, both, both, both, both, P(), P(), P(KVH, CTX))
    return jax.shard_map(
        per_device, mesh=fine, in_specs=placed, out_specs=P(KVH, CTX), check_vma=False
    )
```

```python
import functools
import itertools
import math

import jax
import jax.numpy as jnp
from jax import lax
from jax.experimental import pallas as pl
from jax.experimental.pallas import tpu as pltpu
from jax.sharding import Mesh
from jax.sharding import PartitionSpec as P

HEAD_DIM = 128
GROUP = 8
WINDOWS = 16
TLEN = 32
COLS = TLEN * GROUP
NEG_FILL = -1e30
SCALE = 1.0 / math.sqrt(HEAD_DIM)
LOG2E = math.log2(math.e)

SIZES = {"y": 4, "zb": 2, "za": 2, "core": 2, "zh": 2, "x": 4}
CTX = ("y", "zb", "za", "core")
KVH = ("zh", "x")
CTX_DEVICES = 32
TILE_FLOPS = 16
TOP, TOTAL, STATE_ROWS = HEAD_DIM, HEAD_DIM + 1, HEAD_DIM + 8
VMEM_LIMIT = 48 << 20
SMEM = pl.BlockSpec(memory_space=pltpu.SMEM)
VMEM = pl.BlockSpec(memory_space=pltpu.VMEM)
ANY = pl.BlockSpec(memory_space=pl.ANY)


def move(array, route):
    axes = tuple(route)
    places = list(itertools.product(*[range(SIZES[a]) for a in SIZES]))
    names = list(SIZES)
    pairs = set()
    index = lambda c: functools.reduce(lambda n, a: n * SIZES[a] + c[a], axes, 0)
    for place in places:
        c = dict(zip(names, place))
        pairs.add((index(c), index({a: route[a](c) for a in axes})))
    return lax.ppermute(array, axes, sorted(pairs))


def flip(array, *axes):
    return move(array, {a: (lambda c, a=a: c[a] ^ 1) for a in axes})


def from_y(array, shift):
    return move(array, {"y": lambda c: (c["y"] - shift) % SIZES["y"]})


def after(array, token):
    def kernel(array_ref, token_ref, out_ref):
        pass

    return pl.pallas_call(
        kernel,
        out_shape=jax.ShapeDtypeStruct(array.shape, array.dtype),
        in_specs=[ANY, ANY],
        out_specs=ANY,
        input_output_aliases={0: 0},
        compiler_params=pltpu.CompilerParams(vmem_limit_bytes=1 << 20),
    )(array, token)


def rounded(value):
    return value.astype(jnp.bfloat16).astype(jnp.float32)


def scores(keys, columns):
    return jnp.dot(keys, columns, preferred_element_type=jnp.float32)


def soften(dots, mask=None):
    if mask is not None:
        dots = jnp.where(mask, dots, NEG_FILL)
    top = rounded(jnp.max(dots, axis=0, keepdims=True) * SCALE)
    weights = jnp.exp2(dots * (SCALE * LOG2E) - top * LOG2E)
    if mask is not None:
        weights = jnp.where(mask, weights, 0.0)
    total = rounded(jnp.sum(weights, axis=0, keepdims=True))
    return top, total, weights.astype(jnp.bfloat16)


def block_out(values_t, total, weights):
    out = jnp.dot(values_t, weights, preferred_element_type=jnp.float32)
    return rounded(out * (1.0 / jnp.maximum(total, 0.5)))


def transposed(array):
    return array.astype(jnp.float32).T.astype(jnp.bfloat16)


def absorb(blocks, tiles, seen, columns, states):
    values = {}

    def finish(tile, top, total, weights):
        b, r, e = tile
        out = block_out(values[b], total, weights)
        visible = seen(b, r, e)
        top = jnp.where(visible, top, NEG_FILL)
        total = jnp.where(visible, total, 0.0)
        state_ref = states[r]
        old_top = state_ref[e, TOP : TOP + 1, :]
        joint = jnp.maximum(old_top, top)
        old = jnp.exp(old_top - joint)
        new = jnp.exp(top - joint) * total
        state_ref[e, :HEAD_DIM, :] = old * state_ref[e, :HEAD_DIM, :] + new * out
        state_ref[e, TOTAL : TOTAL + 1, :] = old * state_ref[e, TOTAL : TOTAL + 1, :] + new
        state_ref[e, TOP : TOP + 1, :] = joint

    def start(tile):
        b, r, e = tile
        if b not in values:
            values[b] = transposed(blocks[b][1])
        return scores(blocks[b][0], columns[r][e])

    ahead, behind = start(tiles[0]), None
    for n, tile in enumerate(tiles):
        dots = ahead
        if n + 1 < len(tiles):
            ahead = start(tiles[n + 1])
        softened = soften(dots)
        if behind is not None:
            finish(*behind)
        behind = (tile, *softened)
    finish(*behind)


def sees(meta_ref, select_ref, own_examples, sources):
    y, zb, za, core = [meta_ref[n] for n in range(4)]
    windows = []
    for far_y, far_zb in sources:
        block = (((y + far_y) % 4 * 2 + (zb ^ far_zb)) * 2 + za) * 2 + core
        windows.append(block * WINDOWS // CTX_DEVICES)
    place = ((y * 2 + zb) * 2 + za) * 2 + core

    def seen(b, r, e):
        return select_ref[(place ^ r) * own_examples + e, windows[b]] > 0

    return seen


def make_columns(q_ref, columns_ref):
    for e in range(q_ref.shape[0] // TLEN):
        rows = q_ref[e * TLEN : (e + 1) * TLEN, :]
        stacked = jnp.concatenate(
            [rows[:, h * HEAD_DIM : (h + 1) * HEAD_DIM] for h in range(GROUP)], axis=0
        )
        columns_ref[e] = transposed(stacked)


def own_kernel(meta_ref, select_ref, q_ref, test_ref, kv_ref, columns_ref, state_ref):
    own = q_ref.shape[0] // TLEN
    make_columns(q_ref, columns_ref)
    token = lax.broadcasted_iota(jnp.int32, (TLEN, COLS), 0)
    place = lax.broadcasted_iota(jnp.int32, (TLEN, COLS), 1) % TLEN
    for e in range(own):
        rows = pl.ds(e * TLEN, TLEN)
        dots = scores(test_ref[rows, :HEAD_DIM], columns_ref[e])
        top, total, weights = soften(dots, token <= place)
        out = block_out(transposed(test_ref[rows, HEAD_DIM:]), total, weights)
        state_ref[e, :HEAD_DIM, :] = total * out
        state_ref[e, TOP : TOP + 1, :] = top
        state_ref[e, TOTAL : TOTAL + 1, :] = total
    seen = sees(meta_ref, select_ref, own, [(0, 0)])
    tiles = [(0, 0, e) for e in range(own)]
    absorb([(kv_ref[0], kv_ref[1])], tiles, seen, [columns_ref], [state_ref])


def group_kernel(sources, meta_ref, select_ref, own_columns_ref, own_state_ref, *refs):
    queries, blocks, refs = refs[:3], refs[3 : 3 + len(sources)], refs[3 + len(sources) :]
    weight_ref, others, states, copy_ref, sem = refs[0], refs[1:4], refs[4:8], refs[8], refs[9]
    copy = pltpu.make_async_copy(weight_ref, copy_ref, sem)
    copy.start()
    own = own_state_ref.shape[0]
    states[0][...] = own_state_ref[...]
    empty = lax.broadcasted_iota(jnp.int32, (STATE_ROWS, COLS), 0) == TOP
    for r in range(3):
        make_columns(queries[r], others[r])
        for e in range(own):
            states[r + 1][e] = jnp.where(empty, NEG_FILL, 0.0)
    seen = sees(meta_ref, select_ref, own, sources)
    tiles = [(b, r, e) for b in range(len(blocks)) for r in range(b == 0, 4) for e in range(own)]
    pairs = [(ref[0], ref[1]) for ref in blocks]
    absorb(pairs, tiles, seen, [own_columns_ref, *others], states)
    copy.wait()


def next_kernel(sources, members, skipped, meta_ref, select_ref, *refs):
    count = len(members)
    columns, before = refs[:count], refs[count : 2 * count]
    blocks, states = refs[2 * count : 2 * count + len(sources)], refs[-count:]
    own = before[0].shape[0]
    for n in range(count):
        states[n][...] = before[n][...]
    seen = sees(meta_ref, select_ref, own, sources)
    tiles = [
        (b, n, e)
        for b in range(len(blocks))
        for n in range(count)
        for e in range(own)
        if (b, members[n]) not in skipped
    ]
    pairs = [(ref[0], ref[1]) for ref in blocks]
    absorb(pairs, tiles, lambda b, n, e: seen(b, members[n], e), columns, states)


def joined(parts):
    top = functools.reduce(jnp.maximum, [part[TOP : TOP + 1] for part in parts])
    total, over = 0.0, 0.0
    for part in parts:
        scale = jnp.exp(part[TOP : TOP + 1] - top)
        total = total + scale * part[TOTAL : TOTAL + 1]
        over = over + scale * part[:HEAD_DIM]
    return top, total, over


def join_kernel(far_ref, received_ref, out_ref):
    own = far_ref.shape[0]
    for e in range(own):
        top, total, over = joined([far_ref[e], received_ref[e]])
        out_ref[e, :HEAD_DIM, :] = over
        out_ref[e, TOP : TOP + 1, :] = top
        out_ref[e, TOTAL : TOTAL + 1, :] = total
        out_ref[e, TOTAL + 1 :, :] = jnp.zeros((STATE_ROWS - TOTAL - 1, COLS), jnp.float32)


def finish_kernel(meta_ref, length_ref, mine_ref, received_ref, far_ref, *tokens_and_out):
    out_ref = tokens_and_out[-1]
    own = mine_ref.shape[0]
    place = ((meta_ref[0] * 2 + meta_ref[1]) * 2 + meta_ref[2]) * 2 + meta_ref[3]
    slot = lax.broadcasted_iota(jnp.int32, (1, COLS), 1) % TLEN
    for e in range(own):
        top, total, over = joined([mine_ref[e], received_ref[e], far_ref[e]])
        live = slot < length_ref[place * own + e]
        result = jnp.where(live, over * (1.0 / total), 0.0).T
        for h in range(GROUP):
            out_ref[e * TLEN : (e + 1) * TLEN, h * HEAD_DIM : (h + 1) * HEAD_DIM] = result[
                h * TLEN : (h + 1) * TLEN, :
            ].astype(jnp.bfloat16)


def project_kernel(meta_ref, *refs):
    rows, weights, keep_refs, send_refs, lined_ref = refs[:8], refs[8:12], refs[12:14], refs[14:16], refs[16]
    y, zb, zh, x = [meta_ref[n] for n in (0, 1, 4, 5)]
    height, width = rows[0].shape[0], weights[0].shape[1]
    for n in range(8):
        row_y = (y + n % 4) % 4
        at = ((row_y // 2) ^ zh) * 4 + (x ^ (2 * (row_y % 2) + (zb ^ (n // 4))))
        lined_ref[pl.ds(pl.multiple_of(at * height, height), height), :] = rows[n][...]
    for n in range(4):
        terms = jnp.dot(lined_ref[...], weights[n][...], preferred_element_type=jnp.float32)
        lanes = slice(n * width, (n + 1) * width)
        for h in range(2):
            kept, sent = ((0, 3), (1, 2)) if h == 0 else ((0, 1), (3, 2))
            for d in range(4):
                part = terms[(h * 4 + d) * height : (h * 4 + d + 1) * height]
                if d in kept:
                    keep_refs[h][kept.index(d), :, lanes] = part
                else:
                    send_refs[h][sent.index(d), :, lanes] = part.astype(jnp.bfloat16)


def total_kernel(mine_ref, received_ref, *out_refs):
    width = out_refs[0].shape[1]
    for n in range(4):
        lanes = slice(n * width, (n + 1) * width)
        total = mine_ref[:, lanes] + received_ref[:, lanes].astype(jnp.float32)
        out_refs[n][...] = total.astype(jnp.bfloat16)


def assemble_kernel(meta_ref, *refs):
    out_ref = refs[4]
    height = refs[0].shape[0]
    for n in range(4):
        at = (meta_ref[2] * 2 + meta_ref[3]) ^ n
        out_ref[pl.ds(pl.multiple_of(at * height, height), height), :] = refs[n][...]


def call(kernel, out_shape, inputs, scalars, flops=0, scratch=(), anywhere=0):
    nbytes = sum(a.size * a.dtype.itemsize for a in inputs)
    many = isinstance(out_shape, (list, tuple))
    return pl.pallas_call(
        kernel,
        out_shape=out_shape,
        in_specs=[SMEM] * scalars + [VMEM] * (len(inputs) - scalars - anywhere) + [ANY] * anywhere,
        out_specs=[VMEM] * (len(out_shape) - anywhere) + [ANY] * anywhere if many else VMEM,
        scratch_shapes=list(scratch),
        compiler_params=pltpu.CompilerParams(vmem_limit_bytes=VMEM_LIMIT),
        cost_estimate=pl.CostEstimate(flops=flops, bytes_accessed=nbytes, transcendentals=0),
    )(*inputs)


def per_device(
    queries, cache_keys, cache_values, test_keys, test_values, window_select, test_lengths, out_weight
):
    bf16, f32 = jnp.bfloat16, jnp.float32
    shape = jax.ShapeDtypeStruct
    part = functools.partial
    rows, width = queries.shape
    own = rows // TLEN
    meta = jnp.stack([lax.axis_index(a) for a in SIZES]).astype(jnp.int32)
    scalars = [meta, window_select]
    tile_flops = TILE_FLOPS * COLS * cache_keys.shape[0] * HEAD_DIM
    columns_shape = lambda n: shape((n, HEAD_DIM, COLS), bf16)
    state_shape = lambda n: shape((n, STATE_ROWS, COLS), f32)

    cache = jnp.stack([cache_keys, cache_values])
    cache_z = flip(cache, "zb")
    cache_1, cache_3 = from_y(cache, 1), from_y(cache, 3)
    cache_2 = from_y(cache_1, 1)
    q_far = flip(queries, "za")
    q_near = flip(queries, "core")
    q_far_near = flip(q_far, "core")

    own_columns, own_state = call(
        own_kernel,
        [columns_shape(own), state_shape(own)],
        scalars + [queries, jnp.concatenate([test_keys, test_values], axis=1), cache],
        2,
        2 * own * tile_flops,
    )
    outputs = call(
        part(group_kernel, [(0, 0), (1, 0), (3, 0)]),
        [columns_shape(own)] * 3 + [state_shape(own)] * 4 + [shape(out_weight.shape, bf16)],
        scalars + [own_columns, own_state, q_near, q_far, q_far_near, cache, cache_1, cache_3, out_weight],
        2,
        11 * own * tile_flops,
        scratch=[pltpu.SemaphoreType.DMA],
        anywhere=1,
    )
    columns, states, weight = [own_columns, *outputs[:3]], outputs[3:7], outputs[7]
    cache_z = after(cache_z, states[0])
    cache_z1, cache_z3, cache_z2 = [from_y(cache_z, n) for n in (1, 3, 2)]
    weight_a = flip(weight, "za")

    def next_blocks(states, members, blocks, sources, skipped=(), tokens=()):
        before = [states[r] for r in members]
        after_them = call(
            part(next_kernel, sources, members, skipped),
            [state_shape(own)] * len(members),
            scalars + [columns[r] for r in members] + before + blocks + list(tokens),
            2,
            len(members) * len(blocks) * own * tile_flops,
        )
        for n, r in enumerate(members):
            states[r] = after_them[n]

    blocks, places = [cache_z1, cache_z3, cache_z2], [(1, 1), (3, 1), (2, 1)]
    states = list(states)
    next_blocks(states, (0, 1, 2, 3), [cache_z, cache_2], [(0, 1), (2, 0)])
    next_blocks(states, (2, 3), blocks, places)
    joined_far = call(join_kernel, state_shape(own), [states[2], flip(states[3], "core")], 0)
    received_far = flip(joined_far, "za")
    next_blocks(states, (0, 1), blocks, places, ((2, 0),), [joined_far, weight_a])
    received = flip(states[1], "core")
    next_blocks(states, (0,), blocks[2:], places[2:], (), [received_far])
    attention = call(
        finish_kernel,
        shape(queries.shape, bf16),
        [meta, test_lengths, states[0], received, received_far],
        2,
    )

    weights = [out_weight, flip(out_weight, "core"), weight_a, flip(weight_a, "core")]

    attention_z = flip(attention, "zb")
    rows_all = [a if s == 0 else from_y(a, s) for a in (attention, attention_z) for s in range(4)]
    terms = lambda dtype: shape((2, rows, 4 * out_weight.shape[1]), dtype)
    keep_a, keep_b, send_a, send_b = call(
        project_kernel,
        [terms(f32), terms(f32), terms(bf16), terms(bf16)],
        [meta, *rows_all, *weights],
        1,
        2 * 8 * rows * out_weight.size * 4,
        scratch=[pltpu.VMEM((8 * rows, width), bf16)],
    )
    by_1 = lambda a: move(a, {"x": lambda c: c["x"] ^ 1})
    by_3 = lambda a: move(a, {"x": lambda c: c["x"] ^ 3})
    sum_a = keep_a + by_1(send_a).astype(f32)
    sum_b = keep_b + by_3(send_b).astype(f32)
    sum_a = sum_a[0] + by_3(sum_a[1])
    sum_b = sum_b[0] + by_1(sum_b[1])
    block = shape((rows, out_weight.shape[1]), bf16)
    totals = call(total_kernel, [block] * 4, [sum_a, flip(sum_b.astype(bf16), "zh")], 0)
    arrived = [totals[0], flip(totals[1], "core"), flip(totals[2], "za"), flip(totals[3], "za", "core")]
    return call(assemble_kernel, shape((4 * rows, out_weight.shape[1]), bf16), [meta, *arrived], 1)


def solution(mesh):
    fine = Mesh(mesh.devices.reshape(tuple(SIZES.values())), tuple(SIZES))
    both = P(CTX, KVH)
    placed = (both, both, both, both, both, P(), P(), P(KVH, CTX))
    return jax.shard_map(
        per_device, mesh=fine, in_specs=placed, out_specs=P(KVH, CTX), check_vma=False
    )
```
